32 devices in a mesh: sub: 4 (over y, x), dom: 8 (over z, core).
Axes of the slice: x: 2, y: 2, z: 4, core: 2. Of those that a mesh axis runs over, the one named last changes fastest.
Arguments:
- reduced_basis: bfloat16 [8, 32, 3, 128, 128], P('dom', 'sub'), may hold values from -0.0690534 to 0.0690534
- gauss_stress: float32 [6, 8, 8, 32, 128], P(None, None, 'dom', 'sub'), may hold values from -6 to 6
- yield_flags: int32 [8, 8, 32, 128], P(None, 'dom', 'sub'), may hold values 0 or 1
- consolidation: float32 [8, 8, 32, 128], P(None, 'dom', 'sub'), may hold values from 0.5 to 3
- elastic_moduli: float32 [2, 8, 32, 128], P(None, 'dom', 'sub'), may hold values from 1 to 4
- element_sizes: float32 [3, 8, 32, 128], P(None, 'dom', 'sub'), may hold values from 0.5 to 2
Outputs:
- reduced_tangent: float32 [128, 128], replicated
- reduced_residual: float32 [128], replicated
The draws below stay inside these ranges and needn't reach their ends.
All inputs are finite; a program needn't handle non-finite values. No bound on the sum of `yield_flags` on one device may be relied on, other than what follows from the above.
Results may differ from the reference program's by a relative error of at most 0.00055.
Values may be sent and summed in bfloat16 or wider, within the bound.
No kernel may reach another device: no remote copies, remote signals or barrier semaphores. Data moves between devices by JAX's collectives and lax.ppermute only.
A program may use at most 128 MiB of HBM per device.

```python
import math
import jax
import jax.numpy as jnp
import numpy as np
from jax import lax

NZ = 128
COLS = 128
NX = 8
NY = 32


def draw_reduced_basis(key, part):
    keys = jax.random.split(jax.random.fold_in(key, 7101), 4)
    top_frequency = 2.5
    frequencies = jax.random.uniform(keys[0], (3, 3, COLS), jnp.float32, 0.3, top_frequency)
    phases = jax.random.uniform(keys[1], (3, 3, COLS), jnp.float32, 0.0, 2.0 * math.pi)
    amplitudes = jax.random.uniform(keys[2], (3, COLS), jnp.float32, 0.5, 1.5)
    overall = 5.0 / math.sqrt(NX * NY * NZ)

    def axis_mode(count, axis_index):
        coords = (jnp.arange(count, dtype=jnp.float32) + 0.5) / count
        return jnp.cos(2.0 * math.pi * frequencies[axis_index][None] * coords[:, None, None] + phases[axis_index][None])
    mode_x = axis_mode(NX, 0) * amplitudes[None]
    mode_y = axis_mode(NY, 1)
    mode_z = axis_mode(NZ, 2)

    def one_plane(plane_index):
        factor_x = lax.dynamic_index_in_dim(mode_x, plane_index, 0, False)
        smooth = mode_y[:, None] * mode_z[None, :] * factor_x[None, None]
        plane_key = jax.random.fold_in(keys[3], plane_index)
        noise = jnp.clip(0.05 * jax.random.normal(plane_key, smooth.shape, jnp.float32), -0.2, 0.2)
        plane = (overall * (smooth + noise)).astype(jnp.bfloat16)
        return jnp.transpose(plane, (0, 2, 1, 3))
    return lax.map(one_plane, jnp.arange(NX, dtype=jnp.int32))


def with_ends(result, rng, low, top_value):
    longest = result.shape.index(max(result.shape))
    spots = []
    for shift in (0, 1):
        where = [jax.random.randint(jax.random.fold_in(rng, axis), (), 0, length) for axis, length in enumerate(result.shape)]
        where[longest] = (where[longest] + shift) % result.shape[longest]
        spots.append(tuple(where))
    return result.at[spots[0]].set(low).at[spots[1]].set(top_value)


def shard_levels(stream_key, dims, cuts, smallest, top_value):
    def one(axis_at, blocks):
        steps = jax.random.uniform(jax.random.fold_in(jax.random.fold_in(stream_key, 6), axis_at), (blocks,), jnp.float32, smallest / len(cuts), top_value / len(cuts))
        return jnp.repeat(jnp.exp(steps), dims[axis_at] // blocks).reshape((-1,) + (1,) * (len(dims) - axis_at - 1))

    gain = one(*cuts[0])
    for cut in cuts[1:]:
        gain = gain * one(*cut)
    return gain


def gaussian(rng, extent, width, most, cuts=(), held_as=jnp.bfloat16):
    result = width * jax.random.normal(rng, extent, jnp.float32)
    if cuts:
        result = result * shard_levels(rng, extent, cuts, -0.22, 0.18)
    return jnp.clip(result, -most, most).astype(held_as)


def setup_inputs(seed: int = 0) -> dict:
    key_list = jax.random.split(jax.random.key(seed), 7)
    reduced_basis = draw_reduced_basis(jax.random.fold_in(key_list[6], 71), 0)
    gauss_stress = gaussian(key_list[1], (6, 8, NX, NY, NZ), 1.0, 6.0, ((2, 8), (3, 4)), jnp.float32)
    yield_flags = with_ends((jax.random.randint(key_list[2], (8, NX, NY, NZ), 0, 2) < 1).astype(jnp.int32), jax.random.fold_in(key_list[2], 1), 0, 1)
    consolidation = jnp.clip(jnp.exp(math.log(3.0) - 1.7917595 * jax.random.uniform(key_list[3], (8, NX, NY, NZ), jnp.float32) ** shard_levels(key_list[3], (8, NX, NY, NZ), ((1, 8), (2, 4)), -0.2, 0.2)), 0.5, 3.0)
    elastic_moduli = jnp.clip(jnp.exp(math.log(4.0) - 1.3862944 * jax.random.uniform(key_list[4], (2, NX, NY, NZ), jnp.float32) ** shard_levels(key_list[4], (2, NX, NY, NZ), ((1, 8), (2, 4)), -0.2, 0.2)), 1.0, 4.0)
    element_sizes = jnp.clip(jnp.exp(math.log(2.0) - 1.3862944 * jax.random.uniform(key_list[5], (3, NX, NY, NZ), jnp.float32) ** shard_levels(key_list[5], (3, NX, NY, NZ), ((1, 8), (2, 4)), -0.2, 0.2)), 0.5, 2.0)
    return dict(reduced_basis=reduced_basis, gauss_stress=gauss_stress, yield_flags=yield_flags, consolidation=consolidation, elastic_moduli=elastic_moduli, element_sizes=element_sizes)


GAUSS_POINT = 0.5773502691896258
CRITICAL_SLOPE = 1.2
HARDENING = 0.5
HIGHEST = lax.Precision.HIGHEST


def corner_bits(corner):
    return corner // 4, (corner // 2) % 2, corner % 2


def derivative_table():
    entries = np.zeros((8, 8, 3))
    for gauss_index in range(8):
        gauss_coords = [GAUSS_POINT * (2 * bit_value - 1) for bit_value in corner_bits(gauss_index)]
        for corner in range(8):
            corner_signs = [2 * bit_value - 1 for bit_value in corner_bits(corner)]
            for axis_index in range(3):
                entry_value = float(corner_signs[axis_index])
                for other_axis in range(3):
                    if other_axis != axis_index:
                        entry_value = entry_value * (1.0 + corner_signs[other_axis] * gauss_coords[other_axis]) / 2.0
                entries[gauss_index, corner, axis_index] = entry_value
    return entries


def material(stress_point, flagged, consolidation, bulk_modulus, shear_modulus):
    pressure = -(stress_point[0] + stress_point[1] + stress_point[2]) / 3.0
    deviator_scale = 3.0 / (CRITICAL_SLOPE * CRITICAL_SLOPE)
    volumetric = (2.0 * pressure - consolidation) / 3.0
    normal = [deviator_scale * (stress_point[component] + pressure) - volumetric for component in range(3)]
    normal = normal + [2.0 * deviator_scale * stress_point[component] for component in range(3, 6)]
    lame_first = bulk_modulus - 2.0 / 3.0 * shear_modulus
    normal_trace = normal[0] + normal[1] + normal[2]
    elastic_image = [lame_first * normal_trace + 2.0 * shear_modulus * normal[component] for component in range(3)]
    elastic_image = elastic_image + [shear_modulus * normal[component] for component in range(3, 6)]
    plastic_denominator = HARDENING * consolidation * consolidation
    for component in range(6):
        plastic_denominator = plastic_denominator + normal[component] * elastic_image[component]
    factor = flagged / plastic_denominator
    blank = jnp.zeros_like(bulk_modulus)
    matrix_rows = []
    for row_index in range(6):
        entries = []
        for col_index in range(6):
            if row_index < 3 and col_index < 3:
                elastic = lame_first + (2.0 * shear_modulus if row_index == col_index else blank)
            elif row_index == col_index:
                elastic = shear_modulus
            else:
                elastic = blank
            entries.append(elastic - factor * elastic_image[row_index] * elastic_image[col_index])
        matrix_rows.append(jnp.stack(entries))
    return jnp.stack(matrix_rows)


def element_terms(stress, flags, consolidation, moduli, sizes):
    derivatives = jnp.asarray(derivative_table(), jnp.float32)
    inverse = 1.0 / sizes
    volume = sizes[0] * sizes[1] * sizes[2] / 8.0
    stiffness = None
    nodal_force = None
    for gauss_index in range(8):
        gradients = derivatives[gauss_index][:, :, None, None] * inverse[None]
        blank = jnp.zeros_like(gradients[:, 0])
        along_x, along_y, along_z = gradients[:, 0], gradients[:, 1], gradients[:, 2]
        strain_rows = jnp.stack([
            jnp.stack([along_x, blank, blank], 1),
            jnp.stack([blank, along_y, blank], 1),
            jnp.stack([blank, blank, along_z], 1),
            jnp.stack([along_y, along_x, blank], 1),
            jnp.stack([blank, along_z, along_y], 1),
            jnp.stack([along_z, blank, along_x], 1)])
        stress_point = stress[:, gauss_index]
        tangent = material(stress_point, flags[gauss_index].astype(jnp.float32), consolidation[gauss_index], moduli[0], moduli[1])
        weighted = strain_rows * volume
        stressed = jnp.einsum('klyz,lbjyz->kbjyz', tangent, strain_rows, precision=HIGHEST)
        block_term = jnp.einsum('kaiyz,kbjyz->aibjyz', weighted, stressed, precision=HIGHEST)
        force_term = jnp.einsum('kaiyz,kyz->aiyz', weighted, stress_point, precision=HIGHEST)
        if stiffness is None:
            stiffness, nodal_force = block_term, force_term
        else:
            stiffness, nodal_force = stiffness + block_term, nodal_force + force_term
    return stiffness.astype(jnp.bfloat16), nodal_force


def spread(product, nodal_force):
    planes = [None, None]
    load_planes = [None, None]
    for corner in range(8):
        step_x, step_y, step_z = corner_bits(corner)
        test_rows = jnp.pad(product[corner], ((step_y, 1 - step_y), (step_z, 1 - step_z), (0, 0), (0, 0)))
        nodal_loads = jnp.pad(nodal_force[corner], ((0, 0), (step_y, 1 - step_y), (step_z, 1 - step_z)))
        if planes[step_x] is None:
            planes[step_x], load_planes[step_x] = test_rows, nodal_loads
        else:
            planes[step_x] = planes[step_x] + test_rows
            load_planes[step_x] = load_planes[step_x] + nodal_loads
    return planes[0][:, :-1], load_planes[0][:, :, :-1], planes[1][:, :-1], load_planes[1][:, :, :-1]


def reference(reduced_basis, gauss_stress, yield_flags, consolidation, elastic_moduli, element_sizes):
    reduced_basis = jnp.transpose(reduced_basis, (0, 1, 3, 2, 4))
    columns = reduced_basis.shape[4]

    def layer_step(carried, layer_index):
        tangent, residual, carried_rows, carried_loads = carried
        stiffness, nodal_force = element_terms(
            lax.dynamic_index_in_dim(gauss_stress, layer_index, 2, False),
            lax.dynamic_index_in_dim(yield_flags, layer_index, 1, False),
            lax.dynamic_index_in_dim(consolidation, layer_index, 1, False),
            lax.dynamic_index_in_dim(elastic_moduli, layer_index, 1, False),
            lax.dynamic_index_in_dim(element_sizes, layer_index, 1, False))
        current = lax.dynamic_index_in_dim(reduced_basis, layer_index, 0, False)
        following = lax.dynamic_index_in_dim(reduced_basis, jnp.minimum(layer_index + 1, NX - 1).astype(jnp.int32), 0, False)
        following = jnp.where(layer_index + 1 < NX, following, jnp.zeros_like(following))
        two_planes = jnp.pad(jnp.stack([current, following]), ((0, 0), (0, 1), (0, 1), (0, 0), (0, 0)))
        stacked = jnp.stack([two_planes[corner_bits(corner)[0], corner_bits(corner)[1]:corner_bits(corner)[1] + NY, corner_bits(corner)[2]:corner_bits(corner)[2] + NZ] for corner in range(8)])
        product = jnp.einsum('aibjyz,byzjc->ayzic', stiffness.astype(jnp.float32), stacked.astype(jnp.float32), precision=HIGHEST)
        lower_rows, lower_loads, upper_rows, upper_loads = spread(product, nodal_force)
        test_rows = carried_rows + lower_rows[:NY]
        nodal_loads = carried_loads + lower_loads[:, :NY]
        current_wide = current.astype(jnp.float32)
        tangent = tangent + jnp.einsum('yzic,yzid->cd', current_wide, test_rows, precision=HIGHEST)
        residual = residual + jnp.einsum('yzic,iyz->c', current_wide, nodal_loads, precision=HIGHEST)
        return (tangent, residual, upper_rows[:NY], upper_loads[:, :NY]), None

    initial = (jnp.zeros((columns, columns), jnp.float32), jnp.zeros((columns,), jnp.float32),
               jnp.zeros((NY, NZ, 3, columns), jnp.float32), jnp.zeros((3, NY, NZ), jnp.float32))
    finished, ignored = lax.scan(layer_step, initial, jnp.arange(NX, dtype=jnp.int32))
    return finished[0], finished[1]
```

```python
import functools

import jax
import jax.numpy as jnp
import numpy as np
from jax import lax
from jax.experimental import pallas as pl
from jax.experimental.pallas import tpu as pltpu
from jax.sharding import PartitionSpec as P

GAUSS_POINT = 0.5773502691896258
CRITICAL_SLOPE = 1.2
HARDENING = 0.5
VOIGT = ((0, 3, 5), (3, 1, 4), (5, 4, 2))
LINES = [(x, d) for x in range(2) for d in range(3)]
SAME_PAIRS = [(p, q) for p in range(6) for q in range(p, 6)]
NEXT_PAIRS = [(p, q) for p in range(6) for q in range(6)]
GROUP = 16


def corner_bits(corner):
    return (corner // 4, corner // 2 % 2, corner % 2)


def derivative_table():
    entries = np.zeros((8, 8, 3))
    for gauss_index in range(8):
        gauss_coords = [GAUSS_POINT * (2 * bit_value - 1) for bit_value in corner_bits(gauss_index)]
        for corner in range(8):
            corner_signs = [2 * bit_value - 1 for bit_value in corner_bits(corner)]
            for axis_index in range(3):
                entry_value = float(corner_signs[axis_index])
                for other_axis in range(3):
                    if other_axis != axis_index:
                        entry_value = (
                            entry_value
                            * (1.0 + corner_signs[other_axis] * gauss_coords[other_axis])
                            / 2.0
                        )
                entries[gauss_index, corner, axis_index] = entry_value
    return entries


TABLE = derivative_table()
MOMENTS = np.einsum("gad,gbe->adbe", TABLE, TABLE)


def combine(terms):
    total = None
    for constant, field in terms:
        if abs(constant) < 1e-14:
            continue
        term = field * np.float32(constant)
        total = term if total is None else total + term
    return total


def corner_sums(fields, gauss_index):
    scaled = {}

    def part(i, d, corner):
        constant = TABLE[gauss_index, corner, d]
        key = (i, d, round(abs(constant), 9))
        if key not in scaled:
            scaled[key] = fields[i][d] * np.float32(abs(constant))
        return scaled[key], constant > 0

    sums = []
    for corner in range(8):
        for i in range(3):
            pieces = sorted((part(i, d, corner) for d in range(3)), key=lambda piece: not piece[1])
            total = None
            for value, positive in pieces:
                if total is None:
                    total = value if positive else -value
                else:
                    total = total + value if positive else total - value
            sums.append(total)
    return sums


def stiffness_kernel(
    stress_ref, flags_ref, cons_ref, moduli_ref, sizes_ref, same_ref, next_ref, load_ref, v_ref, w_ref, f_ref
):
    columns, depth = sizes_ref.shape[2], sizes_ref.shape[3]
    sizes = [sizes_ref[d, 0] for d in range(3)]
    inverse = [1.0 / size for size in sizes]
    volume = sizes[0] * sizes[1] * sizes[2] * np.float32(0.125)
    bulk, shear = moduli_ref[0, 0], moduli_ref[1, 0]
    lame = bulk - np.float32(2.0 / 3.0) * shear
    slope = np.float32(3.0 / (CRITICAL_SLOPE * CRITICAL_SLOPE))

    for gauss_index in range(8):
        stress = [stress_ref[k, gauss_index, 0] for k in range(6)]
        cons = cons_ref[gauss_index, 0]
        pressure = (stress[0] + stress[1] + stress[2]) * np.float32(-1.0 / 3.0)
        volumetric = (2.0 * pressure - cons) * np.float32(1.0 / 3.0)
        normal = [slope * (stress[k] + pressure) - volumetric for k in range(3)]
        normal = normal + [(2.0 * slope) * stress[k] for k in range(3, 6)]
        trace = lame * (normal[0] + normal[1] + normal[2])
        twice = 2.0 * shear
        image = [trace + twice * normal[k] for k in range(3)]
        image = image + [shear * normal[k] for k in range(3, 6)]
        denominator = np.float32(HARDENING) * cons * cons
        for k in range(6):
            denominator = denominator + normal[k] * image[k]
        factor = flags_ref[gauss_index, 0].astype(jnp.float32) * volume / denominator
        fields = [[image[VOIGT[i][d]] * inverse[d] for d in range(3)] for i in range(3)]
        for index, value in enumerate(corner_sums(fields, gauss_index)):
            v_ref[gauss_index, index] = value
            w_ref[gauss_index, index] = value * factor
        fields = [[stress[VOIGT[i][d]] * (inverse[d] * volume) for d in range(3)] for i in range(3)]
        for index, value in enumerate(corner_sums(fields, gauss_index)):
            f_ref[index] = value if gauss_index == 0 else f_ref[index] + value

    pair_scale = {}
    for i in range(3):
        for j in range(i, 3):
            scale = volume * inverse[i] * inverse[j]
            pair_scale[i, j] = pair_scale[j, i] = (lame * scale, shear * scale)

    def entry(a, i, b, j):
        terms = [(MOMENTS[a, i, b, j], pair_scale[i, j][0])]
        if i == j:
            for d in range(3):
                weight = MOMENTS[a, d, b, d] + (MOMENTS[a, i, b, i] if d == i else 0.0)
                terms.append((weight, pair_scale[d, d][1]))
        else:
            terms.append((MOMENTS[a, j, b, i], pair_scale[i, j][1]))
        total = combine(terms)
        for gauss_index in range(8):
            term = w_ref[gauss_index, 3 * a + i] * v_ref[gauss_index, 3 * b + j]
            total = -term if total is None else total - term
        return total

    lane = lax.broadcasted_iota(jnp.int32, (columns, depth), 1)
    row = lax.broadcasted_iota(jnp.int32, (columns, depth), 0)

    def along(value):
        return jnp.where(lane == 0, 0.0, pltpu.roll(value, 1, 1))

    def diagonals(p, q, step, other, half):
        (ax, i), (bx, j) = LINES[p], LINES[q]
        a, b = 4 * ax + 2 * step, 4 * bx + 2 * other
        main = entry(a, i, b, j) + along(entry(a + 1, i, b + 1, j))
        after = along(entry(a, i, b + 1, j))
        if half:
            return [main * np.float32(0.5), after]
        return [main, after, entry(a + 1, i, b, j)]

    def store_rows(ref, index, first, second):
        moved = pltpu.roll(second, 1, 0)
        ref[index, 0:columns] = first + jnp.where(row == 0, 0.0, moved)
        ref[index, columns : columns + 1] = moved[0:1]

    index = 0
    for p, q in SAME_PAIRS:
        first = diagonals(p, q, 0, 0, p == q)
        second = diagonals(p, q, 1, 1, p == q)
        for low, high in zip(first, second):
            store_rows(same_ref, index, low, high)
            index += 1
    index = 0
    for p, q in NEXT_PAIRS:
        for value in diagonals(p, q, 0, 1, False):
            next_ref[index] = value
            index += 1
    for p, (x, d) in enumerate(LINES):
        parts = []
        for step in range(2):
            corner = 4 * x + 2 * step
            parts.append(f_ref[3 * corner + d] + along(f_ref[3 * corner + 3 + d]))
        store_rows(load_ref, p, *parts)


def contraction_kernel(
    own_ref, front_ref, side_ref, corner_ref, same_ref, next_ref, load_ref, out_ref,
    basis_ref, turned_ref, blocks_ref, rows_ref, sems,
):
    columns, plane_rows, modes = own_ref.shape
    depth = plane_rows // 3
    group_rows = 2 * plane_rows
    copies = []
    for index, (source, target) in enumerate(
        (
            (own_ref, basis_ref.at[0:columns, 0:plane_rows]),
            (front_ref, basis_ref.at[0:columns, plane_rows:group_rows]),
            (side_ref, basis_ref.at[columns : columns + 1, 0:plane_rows]),
            (corner_ref, basis_ref.at[columns : columns + 1, plane_rows:group_rows]),
        )
    ):
        copy = pltpu.make_async_copy(source, target, sems.at[index])
        copy.start()
        copies.append(copy)

    sub_index = lax.broadcasted_iota(jnp.int32, (GROUP, depth), 0)
    lane = lax.broadcasted_iota(jnp.int32, (GROUP, depth), 1)
    offset = lax.rem(lane - sub_index + depth, GROUP)
    is_main, is_after, is_before = offset == 0, offset == 1, offset == GROUP - 1
    keep = [
        jnp.where(jnp.abs(lane - sub_index - GROUP * r) <= 1, 1.0, 0.0).astype(jnp.bfloat16)
        for r in range(depth // GROUP)
    ]

    def build(row_at, column_at, main, after, before):
        if before is None:
            before = 0.0
        packed = jnp.where(is_main, main, jnp.where(is_after, after, jnp.where(is_before, before, 0.0)))
        packed = packed.astype(jnp.bfloat16)
        for r in range(depth // GROUP):
            blocks_ref[row_at + GROUP * r : row_at + GROUP * (r + 1), column_at : column_at + depth] = (
                packed * keep[r]
            )

    for p in range(6):
        for q in range(p):
            blocks_ref[p * depth : (p + 1) * depth, q * depth : (q + 1) * depth] = jnp.zeros(
                (depth, depth), jnp.bfloat16
            )
    rows_ref[modes : modes + GROUP, :] = jnp.zeros((GROUP, 2 * group_rows), jnp.bfloat16)
    for copy in copies:
        copy.wait()

    def group(y, with_next):
        turned_ref[...] = basis_ref[y].T
        index = 0
        for p, q in SAME_PAIRS:
            count = 2 if p == q else 3
            values = [same_ref[index + k, pl.ds(y, 1), :] for k in range(count)]
            build(p * depth, q * depth, *values, *([None] * (3 - count)))
            index += count
        for n in range(3):
            reach = 2 * (n + 1) * depth
            at = 2 * n * depth
            product = jnp.dot(
                turned_ref[:, 0:reach],
                blocks_ref[0:reach, at : at + 2 * depth],
                preferred_element_type=jnp.float32,
            )
            rows_ref[0:modes, at : at + 2 * depth] = product.astype(jnp.bfloat16)
        for p in range(6):
            value = load_ref[p, pl.ds(y, 1), :]
            leading = value.astype(jnp.bfloat16)
            rest = value - leading.astype(jnp.float32)
            which = lax.broadcasted_iota(jnp.int32, (GROUP, depth), 0)
            rows_ref[modes : modes + GROUP, p * depth : (p + 1) * depth] = jnp.where(
                which == 0, leading.astype(jnp.float32), jnp.where(which == 1, rest, 0.0)
            ).astype(jnp.bfloat16)
        total = jnp.dot(
            rows_ref[:, 0:group_rows], basis_ref[y], preferred_element_type=jnp.float32
        )
        if not with_next:
            return total
        index = 0
        for p, q in NEXT_PAIRS:
            values = [next_ref[index + k, pl.ds(y, 1), :] for k in range(3)]
            build(p * depth, group_rows + q * depth, *values)
            index += 3
        for n in range(3):
            at = group_rows + 2 * n * depth
            product = jnp.dot(
                turned_ref[...],
                blocks_ref[:, at : at + 2 * depth],
                preferred_element_type=jnp.float32,
            )
            rows_ref[0:modes, at : at + 2 * depth] = product.astype(jnp.bfloat16)
        return total + jnp.dot(
            rows_ref[:, group_rows:], basis_ref[y + 1], preferred_element_type=jnp.float32
        )

    out_ref[...] = jnp.zeros_like(out_ref)

    @pl.loop(0, columns)
    def _(y):
        out_ref[...] += group(y, True)

    total = out_ref[...] + group(columns, False)
    upper = total[0:modes]
    out_ref[0:modes] = upper + upper.T
    out_ref[modes:] = total[modes:]


def on_device(
    reduced_basis, gauss_stress, yield_flags, consolidation, elastic_moduli, element_sizes
):
    columns = reduced_basis.shape[1]
    depth, modes = reduced_basis.shape[3], reduced_basis.shape[4]
    plane_rows = 3 * depth
    own = reduced_basis.reshape(columns, plane_rows, modes)
    doms, subs = lax.axis_size("dom"), lax.axis_size("sub")
    front = lax.ppermute(own, "dom", [(s, s - 1) for s in range(1, doms)])
    side = lax.ppermute(own[0:1], "sub", [(s, s - 1) for s in range(1, subs)])
    corner = lax.ppermute(
        own[0:1],
        ("sub", "dom"),
        [(s * doms + t, (s - 1) * doms + t - 1) for s in range(1, subs) for t in range(1, doms)],
    )
    n_same = sum(2 if p == q else 3 for p, q in SAME_PAIRS)
    n_next = 3 * len(NEXT_PAIRS)
    same, following, loads = pl.pallas_call(
        stiffness_kernel,
        out_shape=(
            jax.ShapeDtypeStruct((n_same, 2 * columns, depth), jnp.float32),
            jax.ShapeDtypeStruct((n_next, columns, depth), jnp.float32),
            jax.ShapeDtypeStruct((6, 2 * columns, depth), jnp.float32),
        ),
        scratch_shapes=[
            pltpu.VMEM((8, 24, columns, depth), jnp.float32),
            pltpu.VMEM((8, 24, columns, depth), jnp.float32),
            pltpu.VMEM((24, columns, depth), jnp.float32),
        ],
        compiler_params=pltpu.CompilerParams(vmem_limit_bytes=24 * 2**20),
        cost_estimate=pl.CostEstimate(flops=20_000_000, bytes_accessed=1_500_000, transcendentals=0),
    )(gauss_stress, yield_flags, consolidation, elastic_moduli, element_sizes)
    any_spec = pl.BlockSpec(memory_space=pl.ANY)
    whole = pl.BlockSpec(memory_space=pltpu.VMEM)
    partial = pl.pallas_call(
        contraction_kernel,
        out_shape=jax.ShapeDtypeStruct((modes + GROUP, modes), jnp.float32),
        in_specs=[any_spec] * 4 + [whole] * 3,
        out_specs=whole,
        scratch_shapes=[
            pltpu.VMEM((columns + 1, 2 * plane_rows, modes), jnp.bfloat16),
            pltpu.VMEM((modes, 2 * plane_rows), jnp.bfloat16),
            pltpu.VMEM((2 * plane_rows, 4 * plane_rows), jnp.bfloat16),
            pltpu.VMEM((modes + GROUP, 4 * plane_rows), jnp.bfloat16),
            pltpu.SemaphoreType.DMA((4,)),
        ],
        compiler_params=pltpu.CompilerParams(vmem_limit_bytes=24 * 2**20),
        cost_estimate=pl.CostEstimate(flops=2_000_000_000, bytes_accessed=3_000_000, transcendentals=0),
    )(own, front, side, corner, same, following, loads)

    total = reduce_all(partial)
    return (total[0:modes], total[modes] + total[modes + 1])


def reduce_all(partial):
    subs, doms = lax.axis_size("sub"), lax.axis_size("dom")
    both = ("sub", "dom")
    count = subs * doms
    rows, modes = partial.shape
    short = -(-rows // count) * count
    padded = jnp.pad(partial, ((0, short - rows), (0, 0))).reshape(count, short // count, modes)
    parts = lax.all_to_all(padded, both, 0, 0)
    mine = jnp.sum(parts, axis=0, keepdims=True)
    gathered = lax.all_to_all(jnp.broadcast_to(mine, padded.shape), both, 0, 0)
    return gathered.reshape(short, modes)


def solution(mesh):
    return jax.shard_map(
        on_device,
        mesh=mesh,
        in_specs=(
            P("dom", "sub", None, None, None),
            P(None, None, "dom", "sub", None),
            P(None, "dom", "sub", None),
            P(None, "dom", "sub", None),
            P(None, "dom", "sub", None),
            P(None, "dom", "sub", None),
        ),
        out_specs=(P(), P()),
        check_vma=False,
    )
```

```python
import functools

import jax
import jax.numpy as jnp
import numpy as np
from jax import lax
from jax.experimental import pallas as pl
from jax.experimental.pallas import tpu as pltpu
from jax.sharding import PartitionSpec as P

GAUSS_POINT = 0.5773502691896258
CRITICAL_SLOPE = 1.2
HARDENING = 0.5
VOIGT = ((0, 3, 5), (3, 1, 4), (5, 4, 2))
LINES = [(x, d) for x in range(2) for d in range(3)]
SLOTS = [
    [(0, 0), (0, 1), (0, 2), (0, 3)],
    [(0, 4), (0, 5), (1, 4), (1, 5)],
    [(1, 0), (1, 1), (1, 2), (1, 3)],
]
TILE = 16
PARTS = 4


def corner_bits(corner):
    return (corner // 4, corner // 2 % 2, corner % 2)


def derivative_table():
    entries = np.zeros((8, 8, 3))
    for gauss_index in range(8):
        gauss_coords = [GAUSS_POINT * (2 * bit_value - 1) for bit_value in corner_bits(gauss_index)]
        for corner in range(8):
            corner_signs = [2 * bit_value - 1 for bit_value in corner_bits(corner)]
            for axis_index in range(3):
                entry_value = float(corner_signs[axis_index])
                for other_axis in range(3):
                    if other_axis != axis_index:
                        entry_value = (
                            entry_value
                            * (1.0 + corner_signs[other_axis] * gauss_coords[other_axis])
                            / 2.0
                        )
                entries[gauss_index, corner, axis_index] = entry_value
    return entries


TABLE = derivative_table()
MOMENTS = np.einsum("gad,gbe->adbe", TABLE, TABLE)


def combine(terms):
    total = None
    for constant, field in terms:
        if abs(constant) < 1e-14:
            continue
        term = field * np.float32(constant)
        total = term if total is None else total + term
    return total


def corner_sums(fields, gauss_index):
    scaled = {}

    def part(i, d, corner):
        constant = TABLE[gauss_index, corner, d]
        key = (i, d, round(abs(constant), 9))
        if key not in scaled:
            scaled[key] = fields[i][d] * np.float32(abs(constant))
        return scaled[key], constant > 0

    sums = []
    for corner in range(8):
        for i in range(3):
            pieces = sorted((part(i, d, corner) for d in range(3)), key=lambda piece: not piece[1])
            total = None
            for value, positive in pieces:
                if total is None:
                    total = value if positive else -value
                else:
                    total = total + value if positive else total - value
            sums.append(total)
    return sums


def stiffness_kernel(
    state_ref, blocks_ref,
    v_ref, w_ref, f_ref, field_ref, load_ref, edge_ref,
):
    columns, depth = state_ref.shape[1:]
    flags_at, cons_at, moduli_at, sizes_at = 48, 56, 64, 66
    sizes = [state_ref[sizes_at + d] for d in range(3)]
    inverse = [1.0 / size for size in sizes]
    volume = sizes[0] * sizes[1] * sizes[2] * np.float32(0.125)
    bulk, shear = state_ref[moduli_at], state_ref[moduli_at + 1]
    lame = bulk - np.float32(2.0 / 3.0) * shear
    slope = np.float32(3.0 / (CRITICAL_SLOPE * CRITICAL_SLOPE))

    for gauss_index in range(8):
        stress = [state_ref[8 * k + gauss_index] for k in range(6)]
        cons = state_ref[cons_at + gauss_index]
        pressure = (stress[0] + stress[1] + stress[2]) * np.float32(-1.0 / 3.0)
        volumetric = (2.0 * pressure - cons) * np.float32(1.0 / 3.0)
        normal = [slope * (stress[k] + pressure) - volumetric for k in range(3)]
        normal = normal + [(2.0 * slope) * stress[k] for k in range(3, 6)]
        trace = lame * (normal[0] + normal[1] + normal[2])
        twice = 2.0 * shear
        image = [trace + twice * normal[k] for k in range(3)]
        image = image + [shear * normal[k] for k in range(3, 6)]
        denominator = np.float32(HARDENING) * cons * cons
        for k in range(6):
            denominator = denominator + normal[k] * image[k]
        factor = state_ref[flags_at + gauss_index] * volume / denominator
        fields = [[image[VOIGT[i][d]] * inverse[d] for d in range(3)] for i in range(3)]
        for index, value in enumerate(corner_sums(fields, gauss_index)):
            v_ref[gauss_index, index] = value
            w_ref[gauss_index, index] = value * factor
        fields = [[stress[VOIGT[i][d]] * (inverse[d] * volume) for d in range(3)] for i in range(3)]
        for index, value in enumerate(corner_sums(fields, gauss_index)):
            f_ref[index] = value if gauss_index == 0 else f_ref[index] + value

    pair_scale = {}
    for i in range(3):
        for j in range(i, 3):
            scale = volume * inverse[i] * inverse[j]
            pair_scale[i, j] = pair_scale[j, i] = (lame * scale, shear * scale)

    def entry(a, i, b, j):
        terms = [(MOMENTS[a, i, b, j], pair_scale[i, j][0])]
        if i == j:
            for d in range(3):
                weight = MOMENTS[a, d, b, d] + (MOMENTS[a, i, b, i] if d == i else 0.0)
                terms.append((weight, pair_scale[d, d][1]))
        else:
            terms.append((MOMENTS[a, j, b, i], pair_scale[i, j][1]))
        total = combine(terms)
        for gauss_index in range(8):
            term = w_ref[gauss_index, 3 * a + i] * v_ref[gauss_index, 3 * b + j]
            total = -term if total is None else total - term
        return total

    lane = lax.broadcasted_iota(jnp.int32, (columns, depth), 1)
    row = lax.broadcasted_iota(jnp.int32, (columns, depth), 0)
    zero = jnp.zeros((columns, depth), jnp.float32)
    span = depth // PARTS

    def along(value):
        return jnp.where(lane == 0, 0.0, pltpu.roll(value, 1, 1))

    def diagonals(p, q, step, other):
        (ax, i), (bx, j) = LINES[p], LINES[q]
        a, b = 4 * ax + 2 * step, 4 * bx + 2 * other
        main = entry(a, i, b, j) + along(entry(a + 1, i, b + 1, j))
        after = along(entry(a, i, b + 1, j))
        if step == other and p == q:
            return [main * np.float32(0.5), after, zero]
        return [main, after, jnp.where(lane == depth - 1, 0.0, entry(a + 1, i, b, j))]

    def all_rows(low, high):
        return low + jnp.where(row == 0, 0.0, pltpu.roll(high, 1, 0)), high

    part_of = lane // span

    def regrouped(values):
        moved = [values[0]] + [pltpu.roll(values[q], q * span, 1) for q in range(1, PARTS)]
        parts = []
        for part in range(PARTS):
            merged = moved[-part % PARTS]
            for at in range(1, PARTS):
                merged = jnp.where(part_of == at, moved[(at - part) % PARTS], merged)
            parts.append(pltpu.roll(merged, depth - part * span, 1) if part else merged)
        return parts

    def store(ref, at, kinds):
        for k, pairs in enumerate(kinds):
            firsts = regrouped([zero if pair is None else pair[0] for pair in pairs])
            for part in range(PARTS):
                ref[at + k, part, 0:columns] = firsts[part]
        if all(pair is None or pair[1] is None for pairs in kinds for pair in pairs):
            for k in range(len(kinds)):
                for part in range(PARTS):
                    ref[at + k, part, columns : columns + 1] = zero[0:1]
            return
        lasts = []
        for field in range(PARTS):
            merged = zero
            for k, pairs in enumerate(kinds):
                pair = pairs[field]
                if pair is not None and pair[1] is not None:
                    merged = jnp.where(row == k, pltpu.roll(pair[1], 1 + k, 0), merged)
            lasts.append(merged)
        lasts = regrouped(lasts)
        for k in range(len(kinds)):
            for part in range(PARTS):
                ref[at + k, part, columns : columns + 1] = lasts[part][k : k + 1]

    empty = set()
    for p in range(6):
        for g, slots in enumerate(SLOTS):
            kinds = [[], [], []]
            for following, q in slots:
                if following:
                    values = [(value, None) for value in diagonals(p, q, 0, 1)]
                elif q >= p:
                    low, high = diagonals(p, q, 0, 0), diagonals(p, q, 1, 1)
                    values = [all_rows(low[k], high[k]) for k in range(3)]
                else:
                    values = [None] * 3
                for k in range(3):
                    kinds[k].append(values[k])
            if all(value is None for value in kinds[0]):
                empty.add((p, g))
                continue
            store(field_ref, (p * 3 + g) * 3, kinds)
    loads = []
    for x, d in LINES:
        parts = [f_ref[12 * x + 6 * s + d] + along(f_ref[12 * x + 6 * s + 3 + d]) for s in range(2)]
        loads.append(all_rows(*parts))
    store(load_ref, 0, [loads[0:4], loads[4:6] + [None, None]])

    place = lax.rem(lax.broadcasted_iota(jnp.int32, (span, depth), 1), span)
    offset = (place - lax.broadcasted_iota(jnp.int32, (span, depth), 0)).astype(jnp.bfloat16)
    is_main, is_after, is_before = offset == 0, offset == 1, offset == -1
    begins = place[0:1] == 0
    ends = place[0:1] == span - 1
    tile_row = lax.broadcasted_iota(jnp.int32, (TILE, depth), 0)
    edge_at = 6 * span
    load_at = edge_at + TILE
    edge_ref[...] = jnp.zeros_like(edge_ref)

    @pl.loop(0, columns + 1, unroll=True)
    def _(y):
        for part in range(PARTS):
            at = y * PARTS + part
            for g in range(len(SLOTS)):
                lanes = slice(g * depth, (g + 1) * depth)
                for p in range(6):
                    rows = slice(p * span, (p + 1) * span)
                    if (p, g) in empty:
                        blocks_ref[at, rows, lanes] = jnp.zeros((span, depth), jnp.bfloat16)
                        continue
                    main, after, before = [
                        field_ref[(p * 3 + g) * 3 + k, part, pl.ds(y, 1), :] for k in range(3)
                    ]
                    main16, after16, before16 = [
                        jnp.broadcast_to(value, (TILE, depth)).astype(jnp.bfloat16)
                        for value in (main, after, before)
                    ]
                    for first in range(0, span, TILE):
                        here = slice(first, first + TILE)
                        blocks_ref[at, p * span + first : p * span + first + TILE, lanes] = jnp.where(
                            is_main[here],
                            main16,
                            jnp.where(
                                is_after[here],
                                after16,
                                jnp.where(is_before[here], before16, jnp.bfloat16(0)),
                            ),
                        )
                    edge_ref[p : p + 1, lanes] = jnp.where(begins, after, 0.0)
                    edge_ref[TILE // 2 + p : TILE // 2 + p + 1, lanes] = jnp.where(ends, before, 0.0)
                if g < 2:
                    value = load_ref[g, part, pl.ds(y, 1), :]
                    leading = value.astype(jnp.bfloat16).astype(jnp.float32)
                    blocks_ref[at, load_at : load_at + TILE, lanes] = jnp.where(
                        tile_row == 0, leading, jnp.where(tile_row == 1, value - leading, 0.0)
                    ).astype(jnp.bfloat16)
                else:
                    blocks_ref[at, load_at : load_at + TILE, lanes] = jnp.zeros((TILE, depth), jnp.bfloat16)
            blocks_ref[at, edge_at:load_at] = edge_ref[...].astype(jnp.bfloat16)


def contraction_kernel(
    own_ref, front_ref, side_ref, corner_ref, blocks_ref, mine_ref, other_ref,
    gather_ref, carry_ref, sum_ref, packed_ref,
):
    columns, plane_rows, modes = own_ref.shape
    depth = plane_rows // 3
    span = depth // PARTS
    carry_ref[...] = jnp.zeros_like(carry_ref)
    gather_ref[...] = jnp.zeros_like(gather_ref)
    sum_ref[...] = jnp.zeros_like(sum_ref)
    own_lanes = lax.broadcasted_iota(jnp.int32, (modes, depth), 1) < 2 * span
    nothing = jnp.zeros((8, modes), jnp.float32)

    def group(y, planes):
        def rows(p, first, count):
            ref, at = planes[p // 3]
            start = (p % 3) * depth + first
            return ref[at, start : start + count]

        for border in range(1, PARTS):
            for p in range(6):
                around = rows(p, border * span - TILE, 2 * TILE).astype(jnp.float32)
                at = ((border - 1) * 8 + p) * TILE
                gather_ref[at : at + TILE] = around[TILE // 2 : TILE + TILE // 2]
        total = sum_ref[...]
        for part in range(PARTS):
            before, after = nothing, nothing
            if part > 0:
                before = gather_ref[pl.ds((part - 1) * 8 * TILE + TILE // 2 - 1, 8, TILE)]
            if part < PARTS - 1:
                after = gather_ref[pl.ds(part * 8 * TILE + TILE // 2, 8, TILE)]
            edges = jnp.concatenate([before, after], 0).astype(jnp.bfloat16)
            here = jnp.concatenate([rows(p, part * span, span) for p in range(6)], 0)
            turned = jnp.concatenate([here, edges], 0).T
            at = y * PARTS + part
            product = jnp.dot(
                turned, blocks_ref[at, 0 : 6 * span + TILE], preferred_element_type=jnp.float32
            )
            first = product[:, 0:depth] + carry_ref[part, 0]
            middle = product[:, depth : 2 * depth]
            second = jnp.where(own_lanes, middle + carry_ref[part, 1], 0.0)
            carry_ref[part, 0] = product[:, 2 * depth :]
            carry_ref[part, 1] = pltpu.roll(middle, 2 * span, 1)
            factors = jnp.concatenate([first, second], 1).astype(jnp.bfloat16)
            factors = jnp.concatenate(
                [factors, blocks_ref[at, 6 * span + TILE : 6 * span + 2 * TILE, 0 : 2 * depth]], 0
            )
            total = total + jnp.dot(
                factors[:, 0 : 6 * span], here, preferred_element_type=jnp.float32
            )
        sum_ref[...] = total

    @pl.loop(0, columns, unroll=True)
    def _(y):
        group(y, ((own_ref, y), (front_ref, y)))

    group(columns, ((side_ref, 0), (corner_ref, 0)))
    total = sum_ref[...]
    upper = total[0:modes]
    tangent = upper + upper.T
    half, quarter, share = modes // 2, modes // 4, mine_ref.shape[0]
    packed_ref[0:half] = tangent[0:half]
    packed_ref[half : half + quarter] = jnp.concatenate(
        [tangent[half : half + quarter, half:], tangent[half + quarter :, half:]], 1
    )
    packed_ref[half + quarter :] = jnp.zeros_like(packed_ref[half + quarter :])
    packed_ref[half + quarter : half + quarter + 1] = (
        total[modes : modes + 1] + total[modes + 1 : modes + 2]
    )
    core = lax.rem(lax.axis_index("dom"), 2)
    mine_ref[...] = packed_ref[pl.ds(pl.multiple_of(core * share, 8), share)]
    other_ref[...] = packed_ref[pl.ds(pl.multiple_of((1 - core) * share, 8), share)]


def unpack_kernel(mine_ref, other_ref, tangent_ref, residual_ref, packed_ref):
    share = mine_ref.shape[0]
    modes = tangent_ref.shape[0]
    half, quarter = modes // 2, modes // 4
    core = lax.rem(lax.axis_index("dom"), 2)
    packed_ref[pl.ds(pl.multiple_of(core * share, 8), share)] = mine_ref[...]
    packed_ref[pl.ds(pl.multiple_of((1 - core) * share, 8), share)] = other_ref[...]
    tangent_ref[0:half] = packed_ref[0:half]
    low = packed_ref[half : half + quarter]
    corner = packed_ref[0:half, half:].T
    tangent_ref[half:, 0:half] = corner
    tangent_ref[half : half + quarter, half:] = low[:, 0:half]
    tangent_ref[half + quarter :, half:] = low[:, half:]
    residual_ref[...] = packed_ref[half + quarter : half + quarter + 1]


def on_device(
    reduced_basis, gauss_stress, yield_flags, consolidation, elastic_moduli, element_sizes
):
    columns = reduced_basis.shape[1]
    depth, modes = reduced_basis.shape[3], reduced_basis.shape[4]
    plane_rows = 3 * depth
    own = reduced_basis.reshape(columns, plane_rows, modes)
    doms, subs = lax.axis_size("dom"), lax.axis_size("sub")
    front = lax.ppermute(own, "dom", [(s, s - 1) for s in range(1, doms)])
    first = own[0:1]
    side = lax.ppermute(first, "sub", [(s, s - 1) for s in range(1, subs)])
    corner = lax.ppermute(
        first,
        ("sub", "dom"),
        [(s * doms + t, (s - 1) * doms + t - 1) for s in range(1, subs) for t in range(1, doms)],
    )
    shape = (columns, depth)
    block_rows = 6 * (depth // PARTS) + 2 * TILE
    blocks_shape = ((columns + 1) * PARTS, block_rows, len(SLOTS) * depth)
    fields = [
        value.astype(jnp.float32).reshape((-1,) + shape)
        for value in (gauss_stress, yield_flags, consolidation, elastic_moduli, element_sizes)
    ]
    count = sum(value.shape[0] for value in fields)
    state, at = 0.0, 0
    for value in fields:
        end = at + value.shape[0]
        state = state + jnp.pad(value, ((at, count - end), (0, 0), (0, 0)))
        at = end
    whole = pl.BlockSpec(memory_space=pltpu.VMEM)
    blocks = pl.pallas_call(
        stiffness_kernel,
        out_shape=jax.ShapeDtypeStruct(blocks_shape, jnp.bfloat16),
        in_specs=[whole],
        out_specs=whole,
        scratch_shapes=[
            pltpu.VMEM((8, 24) + shape, jnp.float32),
            pltpu.VMEM((8, 24) + shape, jnp.float32),
            pltpu.VMEM((24,) + shape, jnp.float32),
            pltpu.VMEM((9 * 6, PARTS, 2 * columns, depth), jnp.float32),
            pltpu.VMEM((2, PARTS, 2 * columns, depth), jnp.float32),
            pltpu.VMEM((TILE, len(SLOTS) * depth), jnp.float32),
        ],
        compiler_params=pltpu.CompilerParams(vmem_limit_bytes=24 * 2**20),
        cost_estimate=pl.CostEstimate(flops=20_000_000, bytes_accessed=8_000_000, transcendentals=0),
    )(state)
    packed_rows = -(-(modes // 2 + modes // 4 + 1) // 16) * 16
    share = jax.ShapeDtypeStruct((packed_rows // 2, modes), jnp.float32)
    mine, other = pl.pallas_call(
        contraction_kernel,
        out_shape=(share, share),
        in_specs=[whole] * 5,
        out_specs=(whole, whole),
        scratch_shapes=[
            pltpu.VMEM(((PARTS - 1) * 8 * TILE + TILE, modes), jnp.float32),
            pltpu.VMEM((PARTS, 2, modes, depth), jnp.float32),
            pltpu.VMEM((modes + TILE, modes), jnp.float32),
            pltpu.VMEM((packed_rows, modes), jnp.float32),
        ],
        compiler_params=pltpu.CompilerParams(vmem_limit_bytes=24 * 2**20),
        cost_estimate=pl.CostEstimate(flops=2_000_000_000, bytes_accessed=8_000_000, transcendentals=0),
    )(own, front, side, corner, blocks)

    mine = mine + exchanged(other, "dom", 1)
    for axis, first in (("dom", 2), ("sub", 1)):
        for stride, radix in stages(first, lax.axis_size(axis)):
            received = [exchanged(mine, axis, stride * k) for k in range(radix - 1, 0, -1)]
            mine = sum(received, mine)
    other = exchanged(mine, "dom", 1)
    tangent, residual = pl.pallas_call(
        unpack_kernel,
        out_shape=(
            jax.ShapeDtypeStruct((modes, modes), jnp.float32),
            jax.ShapeDtypeStruct((1, modes), jnp.float32),
        ),
        in_specs=[whole] * 2,
        out_specs=(whole, whole),
        scratch_shapes=[pltpu.VMEM((packed_rows, modes), jnp.float32)],
        compiler_params=pltpu.CompilerParams(vmem_limit_bytes=8 * 2**20),
    )(mine, other)
    return (tangent, residual.reshape(modes))


def exchanged(value, axis, distance):
    return lax.ppermute(value, axis, [(s, s ^ distance) for s in range(lax.axis_size(axis))])


def stages(stride, size):
    found = []
    while stride < size:
        radix = min(4, size // stride)
        found.append((stride, radix))
        stride *= radix
    return found


def solution(mesh):
    return jax.shard_map(
        on_device,
        mesh=mesh,
        in_specs=(
            P("dom", "sub", None, None, None),
            P(None, None, "dom", "sub", None),
            P(None, "dom", "sub", None),
            P(None, "dom", "sub", None),
            P(None, "dom", "sub", None),
            P(None, "dom", "sub", None),
        ),
        out_specs=(P(), P()),
        check_vma=False,
    )
```

```python
import functools

import jax
import jax.numpy as jnp
import numpy as np
from jax import lax
from jax.experimental import pallas as pl
from jax.experimental.pallas import tpu as pltpu
from jax.sharding import PartitionSpec as P

GAUSS_POINT = 0.5773502691896258
CRITICAL_SLOPE = 1.2
HARDENING = 0.5
VOIGT = ((0, 3, 5), (3, 1, 4), (5, 4, 2))
LINES = [(x, d) for x in range(2) for d in range(3)]
SLOTS = [
    [(0, 0), (0, 1), (0, 2), (0, 3)],
    [(0, 4), (0, 5), (1, 4), (1, 5)],
    [(1, 0), (1, 1), (1, 2), (1, 3)],
]
TILE = 16
PARTS = 4


def corner_bits(corner):
    return (corner // 4, corner // 2 % 2, corner % 2)


def derivative_table():
    entries = np.zeros((8, 8, 3))
    for gauss_index in range(8):
        gauss_coords = [GAUSS_POINT * (2 * bit_value - 1) for bit_value in corner_bits(gauss_index)]
        for corner in range(8):
            corner_signs = [2 * bit_value - 1 for bit_value in corner_bits(corner)]
            for axis_index in range(3):
                entry_value = float(corner_signs[axis_index])
                for other_axis in range(3):
                    if other_axis != axis_index:
                        entry_value = (
                            entry_value
                            * (1.0 + corner_signs[other_axis] * gauss_coords[other_axis])
                            / 2.0
                        )
                entries[gauss_index, corner, axis_index] = entry_value
    return entries


TABLE = derivative_table()
MOMENTS = np.einsum("gad,gbe->adbe", TABLE, TABLE)


def combine(terms):
    total = None
    for constant, field in terms:
        if abs(constant) < 1e-14:
            continue
        term = field * np.float32(constant)
        total = term if total is None else total + term
    return total


def corner_sums(fields, gauss_index):
    scaled = {}

    def part(i, d, corner):
        constant = TABLE[gauss_index, corner, d]
        key = (i, d, round(abs(constant), 9))
        if key not in scaled:
            scaled[key] = fields[i][d] * np.float32(abs(constant))
        return scaled[key], constant > 0

    sums = []
    for corner in range(8):
        for i in range(3):
            pieces = sorted((part(i, d, corner) for d in range(3)), key=lambda piece: not piece[1])
            total = None
            for value, positive in pieces:
                if total is None:
                    total = value if positive else -value
                else:
                    total = total + value if positive else total - value
            sums.append(total)
    return sums


def stiffness_kernel(
    state_ref, blocks_ref,
    v_ref, w_ref, f_ref, field_ref, load_ref, edge_ref,
):
    columns, depth = state_ref.shape[1:]
    flags_at, cons_at, moduli_at, sizes_at = 48, 56, 64, 66
    sizes = [state_ref[sizes_at + d] for d in range(3)]
    inverse = [1.0 / size for size in sizes]
    volume = sizes[0] * sizes[1] * sizes[2] * np.float32(0.125)
    bulk, shear = state_ref[moduli_at], state_ref[moduli_at + 1]
    lame = bulk - np.float32(2.0 / 3.0) * shear
    slope = np.float32(3.0 / (CRITICAL_SLOPE * CRITICAL_SLOPE))

    for gauss_index in range(8):
        stress = [state_ref[8 * k + gauss_index] for k in range(6)]
        cons = state_ref[cons_at + gauss_index]
        pressure = (stress[0] + stress[1] + stress[2]) * np.float32(-1.0 / 3.0)
        volumetric = (2.0 * pressure - cons) * np.float32(1.0 / 3.0)
        normal = [slope * (stress[k] + pressure) - volumetric for k in range(3)]
        normal = normal + [(2.0 * slope) * stress[k] for k in range(3, 6)]
        trace = lame * (normal[0] + normal[1] + normal[2])
        twice = 2.0 * shear
        image = [trace + twice * normal[k] for k in range(3)]
        image = image + [shear * normal[k] for k in range(3, 6)]
        denominator = np.float32(HARDENING) * cons * cons
        for k in range(6):
            denominator = denominator + normal[k] * image[k]
        factor = state_ref[flags_at + gauss_index] * volume / denominator
        fields = [[image[VOIGT[i][d]] * inverse[d] for d in range(3)] for i in range(3)]
        for index, value in enumerate(corner_sums(fields, gauss_index)):
            v_ref[gauss_index, index] = value
            w_ref[gauss_index, index] = value * factor
        fields = [[stress[VOIGT[i][d]] * (inverse[d] * volume) for d in range(3)] for i in range(3)]
        for index, value in enumerate(corner_sums(fields, gauss_index)):
            f_ref[index] = value if gauss_index == 0 else f_ref[index] + value

    pair_scale = {}
    for i in range(3):
        for j in range(i, 3):
            scale = volume * inverse[i] * inverse[j]
            pair_scale[i, j] = pair_scale[j, i] = (lame * scale, shear * scale)

    def entry(a, i, b, j):
        terms = [(MOMENTS[a, i, b, j], pair_scale[i, j][0])]
        if i == j:
            for d in range(3):
                weight = MOMENTS[a, d, b, d] + (MOMENTS[a, i, b, i] if d == i else 0.0)
                terms.append((weight, pair_scale[d, d][1]))
        else:
            terms.append((MOMENTS[a, j, b, i], pair_scale[i, j][1]))
        total = combine(terms)
        for gauss_index in range(8):
            term = w_ref[gauss_index, 3 * a + i] * v_ref[gauss_index, 3 * b + j]
            total = -term if total is None else total - term
        return total

    lane = lax.broadcasted_iota(jnp.int32, (columns, depth), 1)
    row = lax.broadcasted_iota(jnp.int32, (columns, depth), 0)
    zero = jnp.zeros((columns, depth), jnp.float32)
    span = depth // PARTS

    def along(value):
        return jnp.where(lane == 0, 0.0, pltpu.roll(value, 1, 1))

    def diagonals(p, q, step, other):
        (ax, i), (bx, j) = LINES[p], LINES[q]
        a, b = 4 * ax + 2 * step, 4 * bx + 2 * other
        main = entry(a, i, b, j) + along(entry(a + 1, i, b + 1, j))
        after = along(entry(a, i, b + 1, j))
        if step == other and p == q:
            return [main * np.float32(0.5), after, zero]
        return [main, after, jnp.where(lane == depth - 1, 0.0, entry(a + 1, i, b, j))]

    def all_rows(low, high):
        return low + jnp.where(row == 0, 0.0, pltpu.roll(high, 1, 0)), high

    part_of = lane // span

    def regrouped(values):
        moved = [values[0]] + [pltpu.roll(values[q], q * span, 1) for q in range(1, PARTS)]
        parts = []
        for part in range(PARTS):
            merged = moved[-part % PARTS]
            for at in range(1, PARTS):
                merged = jnp.where(part_of == at, moved[(at - part) % PARTS], merged)
            parts.append(pltpu.roll(merged, depth - part * span, 1) if part else merged)
        return parts

    def store(ref, at, kinds):
        for k, pairs in enumerate(kinds):
            firsts = regrouped([zero if pair is None else pair[0] for pair in pairs])
            for part in range(PARTS):
                ref[at + k, part, 0:columns] = firsts[part]
        if all(pair is None or pair[1] is None for pairs in kinds for pair in pairs):
            for k in range(len(kinds)):
                for part in range(PARTS):
                    ref[at + k, part, columns : columns + 1] = zero[0:1]
            return
        lasts = []
        for field in range(PARTS):
            merged = zero
            for k, pairs in enumerate(kinds):
                pair = pairs[field]
                if pair is not None and pair[1] is not None:
                    merged = jnp.where(row == k, pltpu.roll(pair[1], 1 + k, 0), merged)
            lasts.append(merged)
        lasts = regrouped(lasts)
        for k in range(len(kinds)):
            for part in range(PARTS):
                ref[at + k, part, columns : columns + 1] = lasts[part][k : k + 1]

    empty = set()
    for p in range(6):
        for g, slots in enumerate(SLOTS):
            kinds = [[], [], []]
            for following, q in slots:
                if following:
                    values = [(value, None) for value in diagonals(p, q, 0, 1)]
                elif q >= p:
                    low, high = diagonals(p, q, 0, 0), diagonals(p, q, 1, 1)
                    values = [all_rows(low[k], high[k]) for k in range(3)]
                else:
                    values = [None] * 3
                for k in range(3):
                    kinds[k].append(values[k])
            if all(value is None for value in kinds[0]):
                empty.add((p, g))
                continue
            store(field_ref, (p * 3 + g) * 3, kinds)
    loads = []
    for x, d in LINES:
        parts = [f_ref[12 * x + 6 * s + d] + along(f_ref[12 * x + 6 * s + 3 + d]) for s in range(2)]
        loads.append(all_rows(*parts))
    store(load_ref, 0, [loads[0:4], loads[4:6] + [None, None]])

    place = lax.rem(lax.broadcasted_iota(jnp.int32, (span, depth), 1), span)
    offset = (place - lax.broadcasted_iota(jnp.int32, (span, depth), 0)).astype(jnp.bfloat16)
    is_main, is_after, is_before = offset == 0, offset == 1, offset == -1
    begins = place[0:1] == 0
    ends = place[0:1] == span - 1
    tile_row = lax.broadcasted_iota(jnp.int32, (TILE, depth), 0)
    edge_at = 6 * span
    load_at = edge_at + TILE
    edge_ref[...] = jnp.zeros_like(edge_ref)

    @pl.loop(0, columns + 1, unroll=True)
    def _(y):
        for part in range(PARTS):
            at = y * PARTS + part
            for g in range(len(SLOTS)):
                lanes = slice(g * depth, (g + 1) * depth)
                for p in range(6):
                    rows = slice(p * span, (p + 1) * span)
                    if (p, g) in empty:
                        blocks_ref[at, rows, lanes] = jnp.zeros((span, depth), jnp.bfloat16)
                        continue
                    main, after, before = [
                        field_ref[(p * 3 + g) * 3 + k, part, pl.ds(y, 1), :] for k in range(3)
                    ]
                    main16, after16, before16 = [
                        jnp.broadcast_to(value, (TILE, depth)).astype(jnp.bfloat16)
                        for value in (main, after, before)
                    ]
                    for first in range(0, span, TILE):
                        here = slice(first, first + TILE)
                        blocks_ref[at, p * span + first : p * span + first + TILE, lanes] = jnp.where(
                            is_main[here],
                            main16,
                            jnp.where(
                                is_after[here],
                                after16,
                                jnp.where(is_before[here], before16, jnp.bfloat16(0)),
                            ),
                        )
                    edge_ref[p : p + 1, lanes] = jnp.where(begins, after, 0.0)
                    edge_ref[TILE // 2 + p : TILE // 2 + p + 1, lanes] = jnp.where(ends, before, 0.0)
                if g < 2:
                    value = load_ref[g, part, pl.ds(y, 1), :]
                    leading = value.astype(jnp.bfloat16).astype(jnp.float32)
                    blocks_ref[at, load_at : load_at + TILE, lanes] = jnp.where(
                        tile_row == 0, leading, jnp.where(tile_row == 1, value - leading, 0.0)
                    ).astype(jnp.bfloat16)
                else:
                    blocks_ref[at, load_at : load_at + TILE, lanes] = jnp.zeros((TILE, depth), jnp.bfloat16)
            blocks_ref[at, edge_at:load_at] = edge_ref[...].astype(jnp.bfloat16)


def contract(y, planes, depth, blocks_ref, gather_ref, carry_ref, sum_ref):
    modes = sum_ref.shape[1]
    span = depth // PARTS
    own_lanes = lax.broadcasted_iota(jnp.int32, (modes, depth), 1) < 2 * span
    nothing = jnp.zeros((8, modes), jnp.float32)

    def rows(p, first, count):
        ref, at = planes[p // 3]
        start = (p % 3) * depth + first
        return ref[at, start : start + count]

    for border in range(1, PARTS):
        for p in range(6):
            around = rows(p, border * span - TILE, 2 * TILE).astype(jnp.float32)
            at = ((border - 1) * 8 + p) * TILE
            gather_ref[at : at + TILE] = around[TILE // 2 : TILE + TILE // 2]
    total = sum_ref[...]
    for part in range(PARTS):
        before, after = nothing, nothing
        if part > 0:
            before = gather_ref[pl.ds((part - 1) * 8 * TILE + TILE // 2 - 1, 8, TILE)]
        if part < PARTS - 1:
            after = gather_ref[pl.ds(part * 8 * TILE + TILE // 2, 8, TILE)]
        edges = jnp.concatenate([before, after], 0).astype(jnp.bfloat16)
        here = jnp.concatenate([rows(p, part * span, span) for p in range(6)], 0)
        turned = jnp.concatenate([here, edges], 0).T
        at = y * PARTS + part
        product = jnp.dot(
            turned, blocks_ref[at, 0 : 6 * span + TILE], preferred_element_type=jnp.float32
        )
        first = product[:, 0:depth] + carry_ref[part, 0]
        middle = product[:, depth : 2 * depth]
        second = jnp.where(own_lanes, middle + carry_ref[part, 1], 0.0)
        carry_ref[part, 0] = product[:, 2 * depth :]
        carry_ref[part, 1] = pltpu.roll(middle, 2 * span, 1)
        factors = jnp.concatenate([first, second], 1).astype(jnp.bfloat16)
        factors = jnp.concatenate(
            [factors, blocks_ref[at, 6 * span + TILE : 6 * span + 2 * TILE, 0 : 2 * depth]], 0
        )
        total = total + jnp.dot(
            factors[:, 0 : 6 * span], here, preferred_element_type=jnp.float32
        )
    sum_ref[...] = total


def contraction_kernel(own_ref, front_ref, blocks_ref, sum_ref, carry_ref, gather_ref):
    columns, plane_rows, modes = own_ref.shape
    carry_ref[...] = jnp.zeros_like(carry_ref)
    gather_ref[...] = jnp.zeros_like(gather_ref)
    sum_ref[...] = jnp.zeros_like(sum_ref)

    @pl.loop(0, columns, unroll=True)
    def _(y):
        planes = ((own_ref, y), (front_ref, y))
        contract(y, planes, plane_rows // 3, blocks_ref, gather_ref, carry_ref, sum_ref)


def last_kernel(
    side_ref, corner_ref, blocks_ref, sum_in, carry_in, mine_ref, other_ref,
    gather_ref, carry_ref, sum_ref, packed_ref, ends_ref,
):
    inside = lax.axis_index("sub") < lax.axis_size("sub") - 1
    ends_ref[0:1] = jnp.where(inside, side_ref[...], jnp.bfloat16(0))
    inside = inside & (lax.axis_index("dom") < lax.axis_size("dom") - 1)
    ends_ref[1:2] = jnp.where(inside, corner_ref[...], jnp.bfloat16(0))
    ignored, plane_rows, modes = side_ref.shape
    columns = blocks_ref.shape[0] // PARTS - 1
    carry_ref[...] = carry_in[...]
    gather_ref[...] = jnp.zeros_like(gather_ref)
    sum_ref[...] = sum_in[...]
    planes = ((ends_ref, 0), (ends_ref, 1))
    contract(columns, planes, plane_rows // 3, blocks_ref, gather_ref, carry_ref, sum_ref)
    total = sum_ref[...]
    upper = total[0:modes]
    tangent = upper + upper.T
    half, quarter, share = modes // 2, modes // 4, mine_ref.shape[0]
    packed_ref[0:half] = tangent[0:half]
    packed_ref[half : half + quarter] = jnp.concatenate(
        [tangent[half : half + quarter, half:], tangent[half + quarter :, half:]], 1
    )
    packed_ref[half + quarter :] = jnp.zeros_like(packed_ref[half + quarter :])
    packed_ref[half + quarter : half + quarter + 1] = (
        total[modes : modes + 1] + total[modes + 1 : modes + 2]
    )
    core = lax.rem(lax.axis_index("dom"), 2)
    mine_ref[...] = packed_ref[pl.ds(pl.multiple_of(core * share, 8), share)]
    other_ref[...] = packed_ref[pl.ds(pl.multiple_of((1 - core) * share, 8), share)]


def unpack_kernel(mine_ref, other_ref, tangent_ref, residual_ref, packed_ref):
    share = mine_ref.shape[0]
    modes = tangent_ref.shape[0]
    half, quarter = modes // 2, modes // 4
    core = lax.rem(lax.axis_index("dom"), 2)
    packed_ref[pl.ds(pl.multiple_of(core * share, 8), share)] = mine_ref[...]
    packed_ref[pl.ds(pl.multiple_of((1 - core) * share, 8), share)] = other_ref[...]
    tangent_ref[0:half] = packed_ref[0:half]
    low = packed_ref[half : half + quarter]
    corner = packed_ref[0:half, half:].T
    tangent_ref[half:, 0:half] = corner
    tangent_ref[half : half + quarter, half:] = low[:, 0:half]
    tangent_ref[half + quarter :, half:] = low[:, half:]
    residual_ref[...] = packed_ref[half + quarter : half + quarter + 1]


def on_device(
    reduced_basis, gauss_stress, yield_flags, consolidation, elastic_moduli, element_sizes
):
    columns = reduced_basis.shape[1]
    depth, modes = reduced_basis.shape[3], reduced_basis.shape[4]
    plane_rows = 3 * depth
    own = reduced_basis.reshape(columns, plane_rows, modes)
    doms, subs = lax.axis_size("dom"), lax.axis_size("sub")
    front = lax.ppermute(own, "dom", [(s, s - 1) for s in range(1, doms)])
    first = own[0:1]
    corner = lax.ppermute(
        first,
        ("sub", "dom"),
        [
            (s * doms + t, (s - 1) % subs * doms + (t - 1) % doms)
            for s in range(subs)
            for t in range(doms)
        ],
    )
    side = lax.ppermute(first, "sub", [(s, (s - 1) % subs) for s in range(subs)])
    shape = (columns, depth)
    block_rows = 6 * (depth // PARTS) + 2 * TILE
    blocks_shape = ((columns + 1) * PARTS, block_rows, len(SLOTS) * depth)
    fields = [
        value.reshape((-1,) + shape)
        for value in (gauss_stress, yield_flags, consolidation, elastic_moduli, element_sizes)
    ]
    count = sum(value.shape[0] for value in fields)
    state, at = 0.0, 0
    for value in fields:
        end = at + value.shape[0]
        state = state + jnp.pad(value, ((at, count - end), (0, 0), (0, 0))).astype(jnp.float32)
        at = end
    whole = pl.BlockSpec(memory_space=pltpu.VMEM)
    blocks = pl.pallas_call(
        stiffness_kernel,
        out_shape=jax.ShapeDtypeStruct(blocks_shape, jnp.bfloat16),
        in_specs=[whole],
        out_specs=whole,
        scratch_shapes=[
            pltpu.VMEM((8, 24) + shape, jnp.float32),
            pltpu.VMEM((8, 24) + shape, jnp.float32),
            pltpu.VMEM((24,) + shape, jnp.float32),
            pltpu.VMEM((9 * 6, PARTS, 2 * columns, depth), jnp.float32),
            pltpu.VMEM((2, PARTS, 2 * columns, depth), jnp.float32),
            pltpu.VMEM((TILE, len(SLOTS) * depth), jnp.float32),
        ],
        compiler_params=pltpu.CompilerParams(vmem_limit_bytes=24 * 2**20),
        cost_estimate=pl.CostEstimate(flops=20_000_000, bytes_accessed=8_000_000, transcendentals=0),
    )(state)
    packed_rows = -(-(modes // 2 + modes // 4 + 1) // 16) * 16
    share = jax.ShapeDtypeStruct((packed_rows // 2, modes), jnp.float32)
    gather_scratch = pltpu.VMEM(((PARTS - 1) * 8 * TILE + TILE, modes), jnp.float32)
    sum_shape = jax.ShapeDtypeStruct((modes + TILE, modes), jnp.float32)
    carry_shape = jax.ShapeDtypeStruct((PARTS, 2, modes, depth), jnp.float32)
    partial, carry = pl.pallas_call(
        contraction_kernel,
        out_shape=(sum_shape, carry_shape),
        in_specs=[whole] * 3,
        out_specs=(whole, whole),
        scratch_shapes=[gather_scratch],
        compiler_params=pltpu.CompilerParams(vmem_limit_bytes=24 * 2**20),
        cost_estimate=pl.CostEstimate(flops=2_000_000_000, bytes_accessed=8_000_000, transcendentals=0),
    )(own, front, blocks)
    mine, other = pl.pallas_call(
        last_kernel,
        out_shape=(share, share),
        in_specs=[whole] * 5,
        out_specs=(whole, whole),
        scratch_shapes=[
            gather_scratch,
            pltpu.VMEM(carry_shape.shape, jnp.float32),
            pltpu.VMEM(sum_shape.shape, jnp.float32),
            pltpu.VMEM((packed_rows, modes), jnp.float32),
            pltpu.VMEM((2, plane_rows, modes), jnp.bfloat16),
        ],
        compiler_params=pltpu.CompilerParams(vmem_limit_bytes=24 * 2**20),
        cost_estimate=pl.CostEstimate(flops=200_000_000, bytes_accessed=1_000_000, transcendentals=0),
    )(side, corner, blocks, partial, carry)

    mine = mine + exchanged(other, "dom", 1)
    for axis, first in (("dom", 2), ("sub", 1)):
        for stride, radix in stages(first, lax.axis_size(axis)):
            received = [exchanged(mine, axis, stride * k) for k in range(radix - 1, 0, -1)]
            mine = sum(received, mine)
    other = exchanged(mine, "dom", 1)
    tangent, residual = pl.pallas_call(
        unpack_kernel,
        out_shape=(
            jax.ShapeDtypeStruct((modes, modes), jnp.float32),
            jax.ShapeDtypeStruct((1, modes), jnp.float32),
        ),
        in_specs=[whole] * 2,
        out_specs=(whole, whole),
        scratch_shapes=[pltpu.VMEM((packed_rows, modes), jnp.float32)],
        compiler_params=pltpu.CompilerParams(vmem_limit_bytes=8 * 2**20),
    )(mine, other)
    return (tangent, residual.reshape(modes))


def exchanged(value, axis, distance):
    return lax.ppermute(value, axis, [(s, s ^ distance) for s in range(lax.axis_size(axis))])


def stages(stride, size):
    found = []
    while stride < size:
        radix = min(4, size // stride)
        found.append((stride, radix))
        stride *= radix
    return found


def solution(mesh):
    return jax.shard_map(
        on_device,
        mesh=mesh,
        in_specs=(
            P("dom", "sub", None, None, None),
            P(None, None, "dom", "sub", None),
            P(None, "dom", "sub", None),
            P(None, "dom", "sub", None),
            P(None, "dom", "sub", None),
            P(None, "dom", "sub", None),
        ),
        out_specs=(P(), P()),
        check_vma=False,
    )
```

```python
import functools

import jax
import jax.numpy as jnp
import numpy as np
from jax import lax
from jax.experimental import pallas as pl
from jax.experimental.pallas import tpu as pltpu
from jax.sharding import PartitionSpec as P

GAUSS_POINT = 0.5773502691896258
CRITICAL_SLOPE = 1.2
HARDENING = 0.5
VOIGT = ((0, 3, 5), (3, 1, 4), (5, 4, 2))
LINES = [(x, d) for x in range(2) for d in range(3)]
SLOTS = [
    [(0, 0), (0, 1), (0, 2), (0, 3)],
    [(0, 4), (0, 5), (1, 4), (1, 5)],
    [(1, 0), (1, 1), (1, 2), (1, 3)],
]
TILE = 16
PARTS = 4


def corner_bits(corner):
    return (corner // 4, corner // 2 % 2, corner % 2)


def derivative_table():
    entries = np.zeros((8, 8, 3))
    for gauss_index in range(8):
        gauss_coords = [GAUSS_POINT * (2 * bit_value - 1) for bit_value in corner_bits(gauss_index)]
        for corner in range(8):
            corner_signs = [2 * bit_value - 1 for bit_value in corner_bits(corner)]
            for axis_index in range(3):
                entry_value = float(corner_signs[axis_index])
                for other_axis in range(3):
                    if other_axis != axis_index:
                        entry_value = (
                            entry_value
                            * (1.0 + corner_signs[other_axis] * gauss_coords[other_axis])
                            / 2.0
                        )
                entries[gauss_index, corner, axis_index] = entry_value
    return entries


TABLE = derivative_table()
MOMENTS = np.einsum("gad,gbe->adbe", TABLE, TABLE)


def combine(terms):
    total = None
    for constant, field in terms:
        if abs(constant) < 1e-14:
            continue
        term = field * np.float32(constant)
        total = term if total is None else total + term
    return total


def corner_sums(fields, gauss_index):
    scaled = {}

    def part(i, d, corner):
        constant = TABLE[gauss_index, corner, d]
        key = (i, d, round(abs(constant), 9))
        if key not in scaled:
            scaled[key] = fields[i][d] * np.float32(abs(constant))
        return scaled[key], constant > 0

    sums = []
    for corner in range(8):
        for i in range(3):
            pieces = sorted((part(i, d, corner) for d in range(3)), key=lambda piece: not piece[1])
            total = None
            for value, positive in pieces:
                if total is None:
                    total = value if positive else -value
                else:
                    total = total + value if positive else total - value
            sums.append(total)
    return sums


def stiffness_kernel(
    state_ref, blocks_ref,
    v_ref, w_ref, f_ref, field_ref, load_ref, edge_ref,
):
    columns, depth = state_ref.shape[1:]
    flags_at, cons_at, moduli_at, sizes_at = 48, 56, 64, 66
    sizes = [state_ref[sizes_at + d] for d in range(3)]
    inverse = [1.0 / size for size in sizes]
    volume = sizes[0] * sizes[1] * sizes[2] * np.float32(0.125)
    bulk, shear = state_ref[moduli_at], state_ref[moduli_at + 1]
    lame = bulk - np.float32(2.0 / 3.0) * shear
    slope = np.float32(3.0 / (CRITICAL_SLOPE * CRITICAL_SLOPE))

    for gauss_index in range(8):
        stress = [state_ref[8 * k + gauss_index] for k in range(6)]
        cons = state_ref[cons_at + gauss_index]
        pressure = (stress[0] + stress[1] + stress[2]) * np.float32(-1.0 / 3.0)
        volumetric = (2.0 * pressure - cons) * np.float32(1.0 / 3.0)
        normal = [slope * (stress[k] + pressure) - volumetric for k in range(3)]
        normal = normal + [(2.0 * slope) * stress[k] for k in range(3, 6)]
        trace = lame * (normal[0] + normal[1] + normal[2])
        twice = 2.0 * shear
        image = [trace + twice * normal[k] for k in range(3)]
        image = image + [shear * normal[k] for k in range(3, 6)]
        denominator = np.float32(HARDENING) * cons * cons
        for k in range(6):
            denominator = denominator + normal[k] * image[k]
        factor = state_ref[flags_at + gauss_index] * volume / denominator
        fields = [[image[VOIGT[i][d]] * inverse[d] for d in range(3)] for i in range(3)]
        for index, value in enumerate(corner_sums(fields, gauss_index)):
            v_ref[gauss_index, index] = value
            w_ref[gauss_index, index] = value * factor
        fields = [[stress[VOIGT[i][d]] * (inverse[d] * volume) for d in range(3)] for i in range(3)]
        for index, value in enumerate(corner_sums(fields, gauss_index)):
            f_ref[index] = value if gauss_index == 0 else f_ref[index] + value

    pair_scale = {}
    for i in range(3):
        for j in range(i, 3):
            scale = volume * inverse[i] * inverse[j]
            pair_scale[i, j] = pair_scale[j, i] = (lame * scale, shear * scale)

    def entry(a, i, b, j):
        terms = [(MOMENTS[a, i, b, j], pair_scale[i, j][0])]
        if i == j:
            for d in range(3):
                weight = MOMENTS[a, d, b, d] + (MOMENTS[a, i, b, i] if d == i else 0.0)
                terms.append((weight, pair_scale[d, d][1]))
        else:
            terms.append((MOMENTS[a, j, b, i], pair_scale[i, j][1]))
        total = combine(terms)
        for gauss_index in range(8):
            term = w_ref[gauss_index, 3 * a + i] * v_ref[gauss_index, 3 * b + j]
            total = -term if total is None else total - term
        return total

    lane = lax.broadcasted_iota(jnp.int32, (columns, depth), 1)
    row = lax.broadcasted_iota(jnp.int32, (columns, depth), 0)
    zero = jnp.zeros((columns, depth), jnp.float32)
    span = depth // PARTS
    live = jnp.where(lax.axis_index("dom") < lax.axis_size("dom") - 1, 1.0, 0.0)

    def along(value):
        return jnp.where(lane == 0, 0.0, pltpu.roll(value, 1, 1))

    def diagonals(p, q, step, other):
        (ax, i), (bx, j) = LINES[p], LINES[q]
        a, b = 4 * ax + 2 * step, 4 * bx + 2 * other
        main = entry(a, i, b, j) + along(entry(a + 1, i, b + 1, j))
        after = along(entry(a, i, b + 1, j))
        if step == other and p == q:
            found = [main * np.float32(0.5), after, zero]
        else:
            found = [main, after, jnp.where(lane == depth - 1, 0.0, entry(a + 1, i, b, j))]
        return [value * live for value in found] if ax or bx else found

    def all_rows(low, high):
        return low + jnp.where(row == 0, 0.0, pltpu.roll(high, 1, 0)), high

    part_of = lane // span

    def regrouped(values):
        moved = [values[0]] + [pltpu.roll(values[q], q * span, 1) for q in range(1, PARTS)]
        parts = []
        for part in range(PARTS):
            merged = moved[-part % PARTS]
            for at in range(1, PARTS):
                merged = jnp.where(part_of == at, moved[(at - part) % PARTS], merged)
            parts.append(pltpu.roll(merged, depth - part * span, 1) if part else merged)
        return parts

    def store(ref, at, kinds):
        for k, pairs in enumerate(kinds):
            firsts = regrouped([zero if pair is None else pair[0] for pair in pairs])
            for part in range(PARTS):
                ref[at + k, part, 0:columns] = firsts[part]
        if all(pair is None or pair[1] is None for pairs in kinds for pair in pairs):
            for k in range(len(kinds)):
                for part in range(PARTS):
                    ref[at + k, part, columns : columns + 1] = zero[0:1]
            return
        lasts = []
        for field in range(PARTS):
            merged = zero
            for k, pairs in enumerate(kinds):
                pair = pairs[field]
                if pair is not None and pair[1] is not None:
                    merged = jnp.where(row == k, pltpu.roll(pair[1], 1 + k, 0), merged)
            lasts.append(merged)
        lasts = regrouped(lasts)
        for k in range(len(kinds)):
            for part in range(PARTS):
                ref[at + k, part, columns : columns + 1] = lasts[part][k : k + 1]

    empty = set()
    for p in range(6):
        for g, slots in enumerate(SLOTS):
            kinds = [[], [], []]
            for following, q in slots:
                if following:
                    values = [(value, None) for value in diagonals(p, q, 0, 1)]
                elif q >= p:
                    low, high = diagonals(p, q, 0, 0), diagonals(p, q, 1, 1)
                    values = [all_rows(low[k], high[k]) for k in range(3)]
                else:
                    values = [None] * 3
                for k in range(3):
                    kinds[k].append(values[k])
            if all(value is None for value in kinds[0]):
                empty.add((p, g))
                continue
            store(field_ref, (p * 3 + g) * 3, kinds)
    loads = []
    for x, d in LINES:
        parts = [f_ref[12 * x + 6 * s + d] + along(f_ref[12 * x + 6 * s + 3 + d]) for s in range(2)]
        loads.append(all_rows(*[part * live for part in parts] if x else parts))
    store(load_ref, 0, [loads[0:4], loads[4:6] + [None, None]])

    place = lax.rem(lax.broadcasted_iota(jnp.int32, (span, depth), 1), span)
    offset = (place - lax.broadcasted_iota(jnp.int32, (span, depth), 0)).astype(jnp.bfloat16)
    is_main, is_after, is_before = offset == 0, offset == 1, offset == -1
    begins = place[0:1] == 0
    ends = place[0:1] == span - 1
    tile_row = lax.broadcasted_iota(jnp.int32, (TILE, depth), 0)
    edge_at = 6 * span
    load_at = edge_at + TILE
    edge_ref[...] = jnp.zeros_like(edge_ref)

    @pl.loop(0, columns + 1, unroll=True)
    def _(y):
        for part in range(PARTS):
            at = y * PARTS + part
            for g in range(len(SLOTS)):
                lanes = slice(g * depth, (g + 1) * depth)
                for p in range(6):
                    rows = slice(p * span, (p + 1) * span)
                    if (p, g) in empty:
                        blocks_ref[at, rows, lanes] = jnp.zeros((span, depth), jnp.bfloat16)
                        continue
                    main, after, before = [
                        field_ref[(p * 3 + g) * 3 + k, part, pl.ds(y, 1), :] for k in range(3)
                    ]
                    main16, after16, before16 = [
                        jnp.broadcast_to(value, (TILE, depth)).astype(jnp.bfloat16)
                        for value in (main, after, before)
                    ]
                    for first in range(0, span, TILE):
                        here = slice(first, first + TILE)
                        blocks_ref[at, p * span + first : p * span + first + TILE, lanes] = jnp.where(
                            is_main[here],
                            main16,
                            jnp.where(
                                is_after[here],
                                after16,
                                jnp.where(is_before[here], before16, jnp.bfloat16(0)),
                            ),
                        )
                    edge_ref[p : p + 1, lanes] = jnp.where(begins, after, 0.0)
                    edge_ref[TILE // 2 + p : TILE // 2 + p + 1, lanes] = jnp.where(ends, before, 0.0)
                if g < 2:
                    value = load_ref[g, part, pl.ds(y, 1), :]
                    leading = value.astype(jnp.bfloat16).astype(jnp.float32)
                    blocks_ref[at, load_at : load_at + TILE, lanes] = jnp.where(
                        tile_row == 0, leading, jnp.where(tile_row == 1, value - leading, 0.0)
                    ).astype(jnp.bfloat16)
                else:
                    blocks_ref[at, load_at : load_at + TILE, lanes] = jnp.zeros((TILE, depth), jnp.bfloat16)
            blocks_ref[at, edge_at:load_at] = edge_ref[...].astype(jnp.bfloat16)


def contract(y, planes, depth, blocks_ref, gather_ref, carry_ref, sum_ref):
    modes = sum_ref.shape[1]
    span = depth // PARTS
    own_lanes = lax.broadcasted_iota(jnp.int32, (modes, depth), 1) < 2 * span
    nothing = jnp.zeros((8, modes), jnp.float32)

    def rows(p, first, count):
        ref, at = planes[p // 3]
        start = (p % 3) * depth + first
        return ref[at, start : start + count]

    for border in range(1, PARTS):
        for p in range(6):
            around = rows(p, border * span - TILE, 2 * TILE).astype(jnp.float32)
            at = ((border - 1) * 8 + p) * TILE
            gather_ref[at : at + TILE] = around[TILE // 2 : TILE + TILE // 2]
    total = sum_ref[...]
    for part in range(PARTS):
        before, after = nothing, nothing
        if part > 0:
            before = gather_ref[pl.ds((part - 1) * 8 * TILE + TILE // 2 - 1, 8, TILE)]
        if part < PARTS - 1:
            after = gather_ref[pl.ds(part * 8 * TILE + TILE // 2, 8, TILE)]
        edges = jnp.concatenate([before, after], 0).astype(jnp.bfloat16)
        here = jnp.concatenate([rows(p, part * span, span) for p in range(6)], 0)
        turned = jnp.concatenate([here, edges], 0).T
        at = y * PARTS + part
        product = jnp.dot(
            turned, blocks_ref[at, 0 : 6 * span + TILE], preferred_element_type=jnp.float32
        )
        first = product[:, 0:depth] + carry_ref[part, 0]
        middle = product[:, depth : 2 * depth]
        second = jnp.where(own_lanes, middle + carry_ref[part, 1], 0.0)
        carry_ref[part, 0] = product[:, 2 * depth :]
        carry_ref[part, 1] = pltpu.roll(middle, 2 * span, 1)
        factors = jnp.concatenate([first, second], 1).astype(jnp.bfloat16)
        factors = jnp.concatenate(
            [factors, blocks_ref[at, 6 * span + TILE : 6 * span + 2 * TILE, 0 : 2 * depth]], 0
        )
        total = total + jnp.dot(
            factors[:, 0 : 6 * span], here, preferred_element_type=jnp.float32
        )
    sum_ref[...] = total


def contraction_kernel(own_ref, front_ref, blocks_ref, sum_ref, carry_ref, gather_ref):
    columns, plane_rows, modes = own_ref.shape
    carry_ref[...] = jnp.zeros_like(carry_ref)
    gather_ref[...] = jnp.zeros_like(gather_ref)
    sum_ref[...] = jnp.zeros_like(sum_ref)

    @pl.loop(0, columns, unroll=True)
    def _(y):
        planes = ((own_ref, y), (front_ref, y))
        contract(y, planes, plane_rows // 3, blocks_ref, gather_ref, carry_ref, sum_ref)


def last_kernel(
    side_ref, corner_ref, blocks_ref, sum_in, carry_in, packed_ref,
    gather_ref, carry_ref, sum_ref, ends_ref,
):
    inside = lax.axis_index("sub") < lax.axis_size("sub") - 1
    ends_ref[0:1] = jnp.where(inside, side_ref[...], jnp.bfloat16(0))
    inside = inside & (lax.axis_index("dom") < lax.axis_size("dom") - 1)
    ends_ref[1:2] = jnp.where(inside, corner_ref[...], jnp.bfloat16(0))
    ignored, plane_rows, modes = side_ref.shape
    columns = blocks_ref.shape[0] // PARTS - 1
    carry_ref[...] = carry_in[...]
    gather_ref[...] = jnp.zeros_like(gather_ref)
    sum_ref[...] = sum_in[...]
    planes = ((ends_ref, 0), (ends_ref, 1))
    contract(columns, planes, plane_rows // 3, blocks_ref, gather_ref, carry_ref, sum_ref)
    total = sum_ref[...]
    upper = total[0:modes]
    tangent = upper + upper.T
    packed_ref[...] = packed(tangent, total[modes : modes + 1] + total[modes + 1 : modes + 2])


def rolled_rows(value, step):
    row = lax.broadcasted_iota(jnp.int32, value.shape, 0)
    result = value
    for j in range(1, value.shape[0]):
        result = jnp.where(row == j, pltpu.roll(value, j * step % value.shape[1], 1), result)
    return result


def packed(tangent, residual):
    modes = tangent.shape[0]
    size = modes // 4
    lane = lax.broadcasted_iota(jnp.int32, (size, modes), 1)
    first, second, third, fourth = [tangent[size * k : size * (k + 1)] for k in range(4)]
    second = jnp.where(lane < size, pltpu.roll(fourth, size, 1), second)
    folded = size // 2
    third = jnp.where(
        lane[:folded] < 2 * size, pltpu.roll(third[folded:], 2 * size, 1), third[:folded]
    )
    count = 2 * modes // size
    spread = rolled_rows(jnp.broadcast_to(residual, (count, modes)), modes - folded)
    middle = jnp.where(lane[:count] < folded, spread, first[folded : folded + count])
    return jnp.concatenate([first[:folded], middle, first[folded + count :], second, third], 0)


def unpack_kernel(mine_ref, other_ref, tangent_ref, residual_ref, packed_ref):
    modes = tangent_ref.shape[0]
    size = modes // 4
    folded = size // 2
    count = 2 * modes // size
    packed_ref[...] = mine_ref[...] + other_ref[...]
    second, third = packed_ref[size : 2 * size], packed_ref[2 * size :]
    upper = jnp.concatenate(
        [
            packed_ref[0 : 2 * size],
            third,
            pltpu.roll(third, 2 * size, 1),
            pltpu.roll(second, modes - size, 1),
        ],
        0,
    )
    lane = lax.broadcasted_iota(jnp.int32, (modes, modes), 1)
    row = lax.broadcasted_iota(jnp.int32, (modes, modes), 0)
    replaced = (row >= folded) & (row < folded + count) & (lane < folded)
    tangent_ref[...] = jnp.where((row // size > lane // size) | replaced, upper.T, upper)
    spread = rolled_rows(packed_ref[folded : folded + count], folded)
    kept = lane[:count] // folded == row[:count]
    residual_ref[...] = jnp.sum(jnp.where(kept, spread, 0.0), axis=0, keepdims=True)


def on_device(
    reduced_basis, gauss_stress, yield_flags, consolidation, elastic_moduli, element_sizes
):
    columns = reduced_basis.shape[1]
    depth, modes = reduced_basis.shape[3], reduced_basis.shape[4]
    plane_rows = 3 * depth
    own = reduced_basis.reshape(columns, plane_rows, modes)
    doms, subs = lax.axis_size("dom"), lax.axis_size("sub")
    front = lax.ppermute(own, "dom", [(s, (s - 1) % doms) for s in range(doms)])
    first = own[0:1]
    corner = lax.ppermute(
        first,
        ("sub", "dom"),
        [
            (s * doms + t, (s - 1) % subs * doms + (t - 1) % doms)
            for s in range(subs)
            for t in range(doms)
        ],
    )
    side = lax.ppermute(first, "sub", [(s, (s - 1) % subs) for s in range(subs)])
    shape = (columns, depth)
    block_rows = 6 * (depth // PARTS) + 2 * TILE
    blocks_shape = ((columns + 1) * PARTS, block_rows, len(SLOTS) * depth)
    fields = [
        value.reshape((-1,) + shape)
        for value in (gauss_stress, yield_flags, consolidation, elastic_moduli, element_sizes)
    ]
    count = sum(value.shape[0] for value in fields)
    state, at = 0.0, 0
    for value in fields:
        end = at + value.shape[0]
        state = state + jnp.pad(value, ((at, count - end), (0, 0), (0, 0))).astype(jnp.float32)
        at = end
    whole = pl.BlockSpec(memory_space=pltpu.VMEM)
    blocks = pl.pallas_call(
        stiffness_kernel,
        out_shape=jax.ShapeDtypeStruct(blocks_shape, jnp.bfloat16),
        in_specs=[whole],
        out_specs=whole,
        scratch_shapes=[
            pltpu.VMEM((8, 24) + shape, jnp.float32),
            pltpu.VMEM((8, 24) + shape, jnp.float32),
            pltpu.VMEM((24,) + shape, jnp.float32),
            pltpu.VMEM((9 * 6, PARTS, 2 * columns, depth), jnp.float32),
            pltpu.VMEM((2, PARTS, 2 * columns, depth), jnp.float32),
            pltpu.VMEM((TILE, len(SLOTS) * depth), jnp.float32),
        ],
        compiler_params=pltpu.CompilerParams(vmem_limit_bytes=24 * 2**20),
        cost_estimate=pl.CostEstimate(flops=20_000_000, bytes_accessed=8_000_000, transcendentals=0),
    )(state)
    packed_rows = modes * 5 // 8
    gather_scratch = pltpu.VMEM(((PARTS - 1) * 8 * TILE + TILE, modes), jnp.float32)
    sum_shape = jax.ShapeDtypeStruct((modes + TILE, modes), jnp.float32)
    carry_shape = jax.ShapeDtypeStruct((PARTS, 2, modes, depth), jnp.float32)
    partial, carry = pl.pallas_call(
        contraction_kernel,
        out_shape=(sum_shape, carry_shape),
        in_specs=[whole] * 3,
        out_specs=(whole, whole),
        scratch_shapes=[gather_scratch],
        compiler_params=pltpu.CompilerParams(vmem_limit_bytes=24 * 2**20),
        cost_estimate=pl.CostEstimate(flops=2_000_000_000, bytes_accessed=8_000_000, transcendentals=0),
    )(own, front, blocks)
    mine = pl.pallas_call(
        last_kernel,
        out_shape=jax.ShapeDtypeStruct((packed_rows, modes), jnp.float32),
        in_specs=[whole] * 5,
        out_specs=whole,
        scratch_shapes=[
            gather_scratch,
            pltpu.VMEM(carry_shape.shape, jnp.float32),
            pltpu.VMEM(sum_shape.shape, jnp.float32),
            pltpu.VMEM((2, plane_rows, modes), jnp.bfloat16),
        ],
        compiler_params=pltpu.CompilerParams(vmem_limit_bytes=24 * 2**20),
        cost_estimate=pl.CostEstimate(flops=200_000_000, bytes_accessed=1_000_000, transcendentals=0),
    )(side, corner, blocks, partial, carry)

    for axis, first in (("sub", 1), ("dom", 2)):
        for stride, radix in stages(first, lax.axis_size(axis)):
            received = [exchanged(mine, axis, stride * k) for k in range(radix - 1, 0, -1)]
            mine = sum(received, mine)
    other = exchanged(mine, "dom", 1)
    tangent, residual = pl.pallas_call(
        unpack_kernel,
        out_shape=(
            jax.ShapeDtypeStruct((modes, modes), jnp.float32),
            jax.ShapeDtypeStruct((1, modes), jnp.float32),
        ),
        in_specs=[whole] * 2,
        out_specs=(whole, whole),
        scratch_shapes=[pltpu.VMEM((packed_rows, modes), jnp.float32)],
        compiler_params=pltpu.CompilerParams(vmem_limit_bytes=8 * 2**20),
    )(mine, other)
    return (tangent, residual.reshape(modes))


def exchanged(value, axis, distance):
    return lax.ppermute(value, axis, [(s, s ^ distance) for s in range(lax.axis_size(axis))])


def stages(stride, size):
    first = stride

    found = []
    while stride < size:
        radix = min(4, size // stride)
        found.append((stride, radix))
        stride *= radix
    return found


def solution(mesh):
    return jax.shard_map(
        on_device,
        mesh=mesh,
        in_specs=(
            P("dom", "sub", None, None, None),
            P(None, None, "dom", "sub", None),
            P(None, "dom", "sub", None),
            P(None, "dom", "sub", None),
            P(None, "dom", "sub", None),
            P(None, "dom", "sub", None),
        ),
        out_specs=(P(), P()),
        check_vma=False,
    )
```

```python
import functools

import jax
import jax.numpy as jnp
import numpy as np
from jax import lax
from jax.experimental import pallas as pl
from jax.experimental.pallas import tpu as pltpu
from jax.sharding import PartitionSpec as P

GAUSS_POINT = 0.5773502691896258
CRITICAL_SLOPE = 1.2
HARDENING = 0.5
VOIGT = ((0, 3, 5), (3, 1, 4), (5, 4, 2))
LINES = [(x, d) for x in range(2) for d in range(3)]
SLOTS = [
    [(0, 0), (0, 1), (0, 2), (0, 3)],
    [(0, 4), (0, 5), (1, 4), (1, 5)],
    [(1, 0), (1, 1), (1, 2), (1, 3)],
]
TILE = 16
PARTS = 4
ORDERS = {2: (1,), 4: (2, 3, 1)}


def corner_bits(corner):
    return (corner // 4, corner // 2 % 2, corner % 2)


def derivative_table():
    entries = np.zeros((8, 8, 3))
    for gauss_index in range(8):
        gauss_coords = [GAUSS_POINT * (2 * bit_value - 1) for bit_value in corner_bits(gauss_index)]
        for corner in range(8):
            corner_signs = [2 * bit_value - 1 for bit_value in corner_bits(corner)]
            for axis_index in range(3):
                entry_value = float(corner_signs[axis_index])
                for other_axis in range(3):
                    if other_axis != axis_index:
                        entry_value = (
                            entry_value
                            * (1.0 + corner_signs[other_axis] * gauss_coords[other_axis])
                            / 2.0
                        )
                entries[gauss_index, corner, axis_index] = entry_value
    return entries


TABLE = derivative_table()
MOMENTS = np.einsum("gad,gbe->adbe", TABLE, TABLE)


def combine(terms):
    total = None
    for constant, field in terms:
        if abs(constant) < 1e-14:
            continue
        term = field * np.float32(constant)
        total = term if total is None else total + term
    return total


def corner_sums(fields, gauss_index):
    scaled = {}

    def part(i, d, corner):
        constant = TABLE[gauss_index, corner, d]
        key = (i, d, round(abs(constant), 9))
        if key not in scaled:
            scaled[key] = fields[i][d] * np.float32(abs(constant))
        return scaled[key], constant > 0

    sums = []
    for corner in range(8):
        for i in range(3):
            pieces = sorted((part(i, d, corner) for d in range(3)), key=lambda piece: not piece[1])
            total = None
            for value, positive in pieces:
                if total is None:
                    total = value if positive else -value
                else:
                    total = total + value if positive else total - value
            sums.append(total)
    return sums


def stiffness_kernel(
    state_ref, blocks_ref,
    v_ref, w_ref, f_ref, field_ref, load_ref, edge_ref,
):
    columns, depth = state_ref.shape[1:]
    flags_at, cons_at, moduli_at, sizes_at = 48, 56, 64, 66
    sizes = [state_ref[sizes_at + d] for d in range(3)]
    inverse = [1.0 / size for size in sizes]
    volume = sizes[0] * sizes[1] * sizes[2] * np.float32(0.125)
    bulk, shear = state_ref[moduli_at], state_ref[moduli_at + 1]
    lame = bulk - np.float32(2.0 / 3.0) * shear
    slope = np.float32(3.0 / (CRITICAL_SLOPE * CRITICAL_SLOPE))

    for gauss_index in range(8):
        stress = [state_ref[8 * k + gauss_index] for k in range(6)]
        cons = state_ref[cons_at + gauss_index]
        pressure = (stress[0] + stress[1] + stress[2]) * np.float32(-1.0 / 3.0)
        volumetric = (2.0 * pressure - cons) * np.float32(1.0 / 3.0)
        normal = [slope * (stress[k] + pressure) - volumetric for k in range(3)]
        normal = normal + [(2.0 * slope) * stress[k] for k in range(3, 6)]
        trace = lame * (normal[0] + normal[1] + normal[2])
        twice = 2.0 * shear
        image = [trace + twice * normal[k] for k in range(3)]
        image = image + [shear * normal[k] for k in range(3, 6)]
        denominator = np.float32(HARDENING) * cons * cons
        for k in range(6):
            denominator = denominator + normal[k] * image[k]
        factor = state_ref[flags_at + gauss_index] * volume / denominator
        fields = [[image[VOIGT[i][d]] * inverse[d] for d in range(3)] for i in range(3)]
        for index, value in enumerate(corner_sums(fields, gauss_index)):
            v_ref[gauss_index, index] = value
            w_ref[gauss_index, index] = value * factor
        fields = [[stress[VOIGT[i][d]] * (inverse[d] * volume) for d in range(3)] for i in range(3)]
        for index, value in enumerate(corner_sums(fields, gauss_index)):
            f_ref[index] = value if gauss_index == 0 else f_ref[index] + value

    pair_scale = {}
    for i in range(3):
        for j in range(i, 3):
            scale = volume * inverse[i] * inverse[j]
            pair_scale[i, j] = pair_scale[j, i] = (lame * scale, shear * scale)

    def entry(a, i, b, j):
        terms = [(MOMENTS[a, i, b, j], pair_scale[i, j][0])]
        if i == j:
            for d in range(3):
                weight = MOMENTS[a, d, b, d] + (MOMENTS[a, i, b, i] if d == i else 0.0)
                terms.append((weight, pair_scale[d, d][1]))
        else:
            terms.append((MOMENTS[a, j, b, i], pair_scale[i, j][1]))
        total = combine(terms)
        for gauss_index in range(8):
            term = w_ref[gauss_index, 3 * a + i] * v_ref[gauss_index, 3 * b + j]
            total = -term if total is None else total - term
        return total

    lane = lax.broadcasted_iota(jnp.int32, (columns, depth), 1)
    row = lax.broadcasted_iota(jnp.int32, (columns, depth), 0)
    zero = jnp.zeros((columns, depth), jnp.float32)
    span = depth // PARTS
    live = jnp.where(lax.axis_index("dom") < lax.axis_size("dom") - 1, 1.0, 0.0)

    def along(value):
        return jnp.where(lane == 0, 0.0, pltpu.roll(value, 1, 1))

    def diagonals(p, q, step, other):
        (ax, i), (bx, j) = LINES[p], LINES[q]
        a, b = 4 * ax + 2 * step, 4 * bx + 2 * other
        main = entry(a, i, b, j) + along(entry(a + 1, i, b + 1, j))
        after = along(entry(a, i, b + 1, j))
        if step == other and p == q:
            found = [main * np.float32(0.5), after, zero]
        else:
            found = [main, after, jnp.where(lane == depth - 1, 0.0, entry(a + 1, i, b, j))]
        return [value * live for value in found] if ax or bx else found

    def all_rows(low, high):
        return low + jnp.where(row == 0, 0.0, pltpu.roll(high, 1, 0)), high

    part_of = lane // span

    def regrouped(values):
        moved = [values[0]] + [pltpu.roll(values[q], q * span, 1) for q in range(1, PARTS)]
        parts = []
        for part in range(PARTS):
            merged = moved[-part % PARTS]
            for at in range(1, PARTS):
                merged = jnp.where(part_of == at, moved[(at - part) % PARTS], merged)
            parts.append(pltpu.roll(merged, depth - part * span, 1) if part else merged)
        return parts

    def store(ref, at, kinds):
        for k, pairs in enumerate(kinds):
            firsts = regrouped([zero if pair is None else pair[0] for pair in pairs])
            for part in range(PARTS):
                ref[at + k, part, 0:columns] = firsts[part]
        if all(pair is None or pair[1] is None for pairs in kinds for pair in pairs):
            for k in range(len(kinds)):
                for part in range(PARTS):
                    ref[at + k, part, columns : columns + 1] = zero[0:1]
            return
        lasts = []
        for field in range(PARTS):
            merged = zero
            for k, pairs in enumerate(kinds):
                pair = pairs[field]
                if pair is not None and pair[1] is not None:
                    merged = jnp.where(row == k, pltpu.roll(pair[1], 1 + k, 0), merged)
            lasts.append(merged)
        lasts = regrouped(lasts)
        for k in range(len(kinds)):
            for part in range(PARTS):
                ref[at + k, part, columns : columns + 1] = lasts[part][k : k + 1]

    empty = set()
    for p in range(6):
        for g, slots in enumerate(SLOTS):
            kinds = [[], [], []]
            for following, q in slots:
                if following:
                    values = [(value, None) for value in diagonals(p, q, 0, 1)]
                elif q >= p:
                    low, high = diagonals(p, q, 0, 0), diagonals(p, q, 1, 1)
                    values = [all_rows(low[k], high[k]) for k in range(3)]
                else:
                    values = [None] * 3
                for k in range(3):
                    kinds[k].append(values[k])
            if all(value is None for value in kinds[0]):
                empty.add((p, g))
                continue
            store(field_ref, (p * 3 + g) * 3, kinds)
    loads = []
    for x, d in LINES:
        parts = [f_ref[12 * x + 6 * s + d] + along(f_ref[12 * x + 6 * s + 3 + d]) for s in range(2)]
        loads.append(all_rows(*[part * live for part in parts] if x else parts))
    store(load_ref, 0, [loads[0:4], loads[4:6] + [None, None]])

    place = lax.rem(lax.broadcasted_iota(jnp.int32, (span, depth), 1), span)
    offset = (place - lax.broadcasted_iota(jnp.int32, (span, depth), 0)).astype(jnp.bfloat16)
    is_main, is_after, is_before = offset == 0, offset == 1, offset == -1
    begins = place[0:1] == 0
    ends = place[0:1] == span - 1
    tile_row = lax.broadcasted_iota(jnp.int32, (TILE, depth), 0)
    edge_at = 6 * span
    load_at = edge_at + TILE
    edge_ref[...] = jnp.zeros_like(edge_ref)

    @pl.loop(0, columns + 1, unroll=True)
    def _(y):
        for part in range(PARTS):
            at = y * PARTS + part
            for g in range(len(SLOTS)):
                lanes = slice(g * depth, (g + 1) * depth)
                for p in range(6):
                    rows = slice(p * span, (p + 1) * span)
                    if (p, g) in empty:
                        blocks_ref[at, rows, lanes] = jnp.zeros((span, depth), jnp.bfloat16)
                        continue
                    main, after, before = [
                        field_ref[(p * 3 + g) * 3 + k, part, pl.ds(y, 1), :] for k in range(3)
                    ]
                    main16, after16, before16 = [
                        jnp.broadcast_to(value, (TILE, depth)).astype(jnp.bfloat16)
                        for value in (main, after, before)
                    ]
                    for first in range(0, span, TILE):
                        here = slice(first, first + TILE)
                        blocks_ref[at, p * span + first : p * span + first + TILE, lanes] = jnp.where(
                            is_main[here],
                            main16,
                            jnp.where(
                                is_after[here],
                                after16,
                                jnp.where(is_before[here], before16, jnp.bfloat16(0)),
                            ),
                        )
                    edge_ref[p : p + 1, lanes] = jnp.where(begins, after, 0.0)
                    edge_ref[TILE // 2 + p : TILE // 2 + p + 1, lanes] = jnp.where(ends, before, 0.0)
                if g < 2:
                    value = load_ref[g, part, pl.ds(y, 1), :]
                    leading = value.astype(jnp.bfloat16).astype(jnp.float32)
                    blocks_ref[at, load_at : load_at + TILE, lanes] = jnp.where(
                        tile_row == 0, leading, jnp.where(tile_row == 1, value - leading, 0.0)
                    ).astype(jnp.bfloat16)
                else:
                    blocks_ref[at, load_at : load_at + TILE, lanes] = jnp.zeros((TILE, depth), jnp.bfloat16)
            blocks_ref[at, edge_at:load_at] = edge_ref[...].astype(jnp.bfloat16)


def contract(y, planes, depth, blocks_ref, gather_ref, carry_ref, sum_ref):
    modes = sum_ref.shape[1]
    span = depth // PARTS
    own_lanes = lax.broadcasted_iota(jnp.int32, (modes, depth), 1) < 2 * span
    nothing = jnp.zeros((8, modes), jnp.float32)

    def rows(p, first, count):
        ref, at = planes[p // 3]
        start = (p % 3) * depth + first
        return ref[at, start : start + count]

    for border in range(1, PARTS):
        for p in range(6):
            around = rows(p, border * span - TILE, 2 * TILE).astype(jnp.float32)
            at = ((border - 1) * 8 + p) * TILE
            gather_ref[at : at + TILE] = around[TILE // 2 : TILE + TILE // 2]
    total = sum_ref[...]
    for part in range(PARTS):
        before, after = nothing, nothing
        if part > 0:
            before = gather_ref[pl.ds((part - 1) * 8 * TILE + TILE // 2 - 1, 8, TILE)]
        if part < PARTS - 1:
            after = gather_ref[pl.ds(part * 8 * TILE + TILE // 2, 8, TILE)]
        edges = jnp.concatenate([before, after], 0).astype(jnp.bfloat16)
        here = jnp.concatenate([rows(p, part * span, span) for p in range(6)], 0)
        turned = jnp.concatenate([here, edges], 0).T
        at = y * PARTS + part
        product = jnp.dot(
            turned, blocks_ref[at, 0 : 6 * span + TILE], preferred_element_type=jnp.float32
        )
        first = product[:, 0:depth] + carry_ref[part, 0]
        middle = product[:, depth : 2 * depth]
        second = jnp.where(own_lanes, middle + carry_ref[part, 1], 0.0)
        carry_ref[part, 0] = product[:, 2 * depth :]
        carry_ref[part, 1] = pltpu.roll(middle, 2 * span, 1)
        factors = jnp.concatenate([first, second], 1).astype(jnp.bfloat16)
        factors = jnp.concatenate(
            [factors, blocks_ref[at, 6 * span + TILE : 6 * span + 2 * TILE, 0 : 2 * depth]], 0
        )
        total = total + jnp.dot(
            factors[:, 0 : 6 * span], here, preferred_element_type=jnp.float32
        )
    sum_ref[...] = total


def contraction_kernel(own_ref, front_ref, blocks_ref, sum_ref, carry_ref, gather_ref):
    columns, plane_rows, modes = own_ref.shape
    carry_ref[...] = jnp.zeros_like(carry_ref)
    gather_ref[...] = jnp.zeros_like(gather_ref)
    sum_ref[...] = jnp.zeros_like(sum_ref)

    @pl.loop(0, columns, unroll=True)
    def _(y):
        planes = ((own_ref, y), (front_ref, y))
        contract(y, planes, plane_rows // 3, blocks_ref, gather_ref, carry_ref, sum_ref)


def last_kernel(
    side_ref, corner_ref, blocks_ref, sum_in, carry_in, packed_ref,
    gather_ref, carry_ref, sum_ref, ends_ref,
):
    inside = lax.axis_index("sub") < lax.axis_size("sub") - 1
    ends_ref[0:1] = jnp.where(inside, side_ref[...], jnp.bfloat16(0))
    inside = inside & (lax.axis_index("dom") < lax.axis_size("dom") - 1)
    ends_ref[1:2] = jnp.where(inside, corner_ref[...], jnp.bfloat16(0))
    ignored, plane_rows, modes = side_ref.shape
    columns = blocks_ref.shape[0] // PARTS - 1
    carry_ref[...] = carry_in[...]
    gather_ref[...] = jnp.zeros_like(gather_ref)
    sum_ref[...] = sum_in[...]
    planes = ((ends_ref, 0), (ends_ref, 1))
    contract(columns, planes, plane_rows // 3, blocks_ref, gather_ref, carry_ref, sum_ref)
    total = sum_ref[...]
    upper = total[0:modes]
    tangent = upper + upper.T
    packed_ref[...] = packed(tangent, total[modes : modes + 1] + total[modes + 1 : modes + 2])


def rolled_rows(value, step):
    row = lax.broadcasted_iota(jnp.int32, value.shape, 0)
    result = value
    for j in range(1, value.shape[0]):
        result = jnp.where(row == j, pltpu.roll(value, j * step % value.shape[1], 1), result)
    return result


def packed(tangent, residual):
    modes = tangent.shape[0]
    size = modes // 4
    lane = lax.broadcasted_iota(jnp.int32, (size, modes), 1)
    first, second, third, fourth = [tangent[size * k : size * (k + 1)] for k in range(4)]
    second = jnp.where(lane < size, pltpu.roll(fourth, size, 1), second)
    folded = size // 2
    third = jnp.where(
        lane[:folded] < 2 * size, pltpu.roll(third[folded:], 2 * size, 1), third[:folded]
    )
    count = 2 * modes // size
    spread = rolled_rows(jnp.broadcast_to(residual, (count, modes)), modes - folded)
    middle = jnp.where(lane[:count] < folded, spread, first[folded : folded + count])
    return jnp.concatenate([first[:folded], middle, first[folded + count :], second, third], 0)


def unpack_kernel(mine_ref, other_ref, tangent_ref, residual_ref, packed_ref):
    modes = tangent_ref.shape[0]
    size = modes // 4
    folded = size // 2
    count = 2 * modes // size
    packed_ref[...] = mine_ref[...] + other_ref[...]
    second, third = packed_ref[size : 2 * size], packed_ref[2 * size :]
    upper = jnp.concatenate(
        [
            packed_ref[0 : 2 * size],
            third,
            pltpu.roll(third, 2 * size, 1),
            pltpu.roll(second, modes - size, 1),
        ],
        0,
    )
    lane = lax.broadcasted_iota(jnp.int32, (modes, modes), 1)
    row = lax.broadcasted_iota(jnp.int32, (modes, modes), 0)
    replaced = (row >= folded) & (row < folded + count) & (lane < folded)
    tangent_ref[...] = jnp.where((row // size > lane // size) | replaced, upper.T, upper)
    spread = rolled_rows(packed_ref[folded : folded + count], folded)
    kept = lane[:count] // folded == row[:count]
    residual_ref[...] = jnp.sum(jnp.where(kept, spread, 0.0), axis=0, keepdims=True)


def on_device(
    reduced_basis, gauss_stress, yield_flags, consolidation, elastic_moduli, element_sizes
):
    columns = reduced_basis.shape[1]
    depth, modes = reduced_basis.shape[3], reduced_basis.shape[4]
    plane_rows = 3 * depth
    own = reduced_basis.reshape(columns, plane_rows, modes)
    doms, subs = lax.axis_size("dom"), lax.axis_size("sub")
    front = lax.ppermute(own, "dom", [(s, (s - 1) % doms) for s in range(doms)])
    first = own[0:1]
    corner = lax.ppermute(
        first,
        ("sub", "dom"),
        [
            (s * doms + t, (s - 1) % subs * doms + (t - 1) % doms)
            for s in range(subs)
            for t in range(doms)
        ],
    )
    side = lax.ppermute(first, "sub", [(s, (s - 1) % subs) for s in range(subs)])
    shape = (columns, depth)
    block_rows = 6 * (depth // PARTS) + 2 * TILE
    blocks_shape = ((columns + 1) * PARTS, block_rows, len(SLOTS) * depth)
    fields = [
        value.reshape((-1,) + shape)
        for value in (gauss_stress, yield_flags, consolidation, elastic_moduli, element_sizes)
    ]
    count = sum(value.shape[0] for value in fields)
    state, at = 0.0, 0
    for value in fields:
        end = at + value.shape[0]
        state = state + jnp.pad(value, ((at, count - end), (0, 0), (0, 0))).astype(jnp.float32)
        at = end
    whole = pl.BlockSpec(memory_space=pltpu.VMEM)
    blocks = pl.pallas_call(
        stiffness_kernel,
        out_shape=jax.ShapeDtypeStruct(blocks_shape, jnp.bfloat16),
        in_specs=[whole],
        out_specs=whole,
        scratch_shapes=[
            pltpu.VMEM((8, 24) + shape, jnp.float32),
            pltpu.VMEM((8, 24) + shape, jnp.float32),
            pltpu.VMEM((24,) + shape, jnp.float32),
            pltpu.VMEM((9 * 6, PARTS, 2 * columns, depth), jnp.float32),
            pltpu.VMEM((2, PARTS, 2 * columns, depth), jnp.float32),
            pltpu.VMEM((TILE, len(SLOTS) * depth), jnp.float32),
        ],
        compiler_params=pltpu.CompilerParams(vmem_limit_bytes=24 * 2**20),
        cost_estimate=pl.CostEstimate(flops=20_000_000, bytes_accessed=8_000_000, transcendentals=0),
    )(state)
    packed_rows = modes * 5 // 8
    gather_scratch = pltpu.VMEM(((PARTS - 1) * 8 * TILE + TILE, modes), jnp.float32)
    sum_shape = jax.ShapeDtypeStruct((modes + TILE, modes), jnp.float32)
    carry_shape = jax.ShapeDtypeStruct((PARTS, 2, modes, depth), jnp.float32)
    partial, carry = pl.pallas_call(
        contraction_kernel,
        out_shape=(sum_shape, carry_shape),
        in_specs=[whole] * 3,
        out_specs=(whole, whole),
        scratch_shapes=[gather_scratch],
        compiler_params=pltpu.CompilerParams(vmem_limit_bytes=24 * 2**20),
        cost_estimate=pl.CostEstimate(flops=2_000_000_000, bytes_accessed=8_000_000, transcendentals=0),
    )(own, front, blocks)
    mine = pl.pallas_call(
        last_kernel,
        out_shape=jax.ShapeDtypeStruct((packed_rows, modes), jnp.float32),
        in_specs=[whole] * 5,
        out_specs=whole,
        scratch_shapes=[
            gather_scratch,
            pltpu.VMEM(carry_shape.shape, jnp.float32),
            pltpu.VMEM(sum_shape.shape, jnp.float32),
            pltpu.VMEM((2, plane_rows, modes), jnp.bfloat16),
        ],
        compiler_params=pltpu.CompilerParams(vmem_limit_bytes=24 * 2**20),
        cost_estimate=pl.CostEstimate(flops=200_000_000, bytes_accessed=1_000_000, transcendentals=0),
    )(side, corner, blocks, partial, carry)

    for axis, first in (("sub", 1), ("dom", 2)):
        for stride, radix in stages(first, lax.axis_size(axis)):
            received = [exchanged(mine, axis, stride * k) for k in ORDERS[radix]]
            mine = sum(received, mine)
    other = exchanged(mine, "dom", 1)
    tangent, residual = pl.pallas_call(
        unpack_kernel,
        out_shape=(
            jax.ShapeDtypeStruct((modes, modes), jnp.float32),
            jax.ShapeDtypeStruct((1, modes), jnp.float32),
        ),
        in_specs=[whole] * 2,
        out_specs=(whole, whole),
        scratch_shapes=[pltpu.VMEM((packed_rows, modes), jnp.float32)],
        compiler_params=pltpu.CompilerParams(vmem_limit_bytes=8 * 2**20),
    )(mine, other)
    return (tangent, residual.reshape(modes))


def exchanged(value, axis, distance):
    return lax.ppermute(value, axis, [(s, s ^ distance) for s in range(lax.axis_size(axis))])


def stages(stride, size):
    first = stride

    found = []
    while stride < size:
        radix = min(4, size // stride)
        found.append((stride, radix))
        stride *= radix
    return found


def solution(mesh):
    return jax.shard_map(
        on_device,
        mesh=mesh,
        in_specs=(
            P("dom", "sub", None, None, None),
            P(None, None, "dom", "sub", None),
            P(None, "dom", "sub", None),
            P(None, "dom", "sub", None),
            P(None, "dom", "sub", None),
            P(None, "dom", "sub", None),
        ),
        out_specs=(P(), P()),
        check_vma=False,
    )
```

```python
import functools

import jax
import jax.numpy as jnp
import numpy as np
from jax import lax
from jax.experimental import pallas as pl
from jax.experimental.pallas import tpu as pltpu
from jax.sharding import PartitionSpec as P

GAUSS_POINT = 0.5773502691896258
CRITICAL_SLOPE = 1.2
HARDENING = 0.5
VOIGT = ((0, 3, 5), (3, 1, 4), (5, 4, 2))
LINES = [(x, d) for x in range(2) for d in range(3)]
SLOTS = [
    [(0, 0), (0, 1), (0, 2), (0, 3)],
    [(0, 4), (0, 5), (1, 4), (1, 5)],
    [(1, 0), (1, 1), (1, 2), (1, 3)],
]
TILE = 16
PARTS = 4
ORDERS = {("sub", 2): (1,), ("sub", 4): (3, 1, 2), ("dom", 2): (1,), ("dom", 4): (2, 3, 1)}


def corner_bits(corner):
    return (corner // 4, corner // 2 % 2, corner % 2)


def derivative_table():
    entries = np.zeros((8, 8, 3))
    for gauss_index in range(8):
        gauss_coords = [GAUSS_POINT * (2 * bit_value - 1) for bit_value in corner_bits(gauss_index)]
        for corner in range(8):
            corner_signs = [2 * bit_value - 1 for bit_value in corner_bits(corner)]
            for axis_index in range(3):
                entry_value = float(corner_signs[axis_index])
                for other_axis in range(3):
                    if other_axis != axis_index:
                        entry_value = (
                            entry_value
                            * (1.0 + corner_signs[other_axis] * gauss_coords[other_axis])
                            / 2.0
                        )
                entries[gauss_index, corner, axis_index] = entry_value
    return entries


TABLE = derivative_table()
MOMENTS = np.einsum("gad,gbe->adbe", TABLE, TABLE)


def combine(terms):
    total = None
    for constant, field in terms:
        if abs(constant) < 1e-14:
            continue
        term = field * np.float32(constant)
        total = term if total is None else total + term
    return total


def corner_sums(fields, gauss_index):
    scaled = {}

    def part(i, d, corner):
        constant = TABLE[gauss_index, corner, d]
        key = (i, d, round(abs(constant), 9))
        if key not in scaled:
            scaled[key] = fields[i][d] * np.float32(abs(constant))
        return scaled[key], constant > 0

    sums = []
    for corner in range(8):
        for i in range(3):
            pieces = sorted((part(i, d, corner) for d in range(3)), key=lambda piece: not piece[1])
            total = None
            for value, positive in pieces:
                if total is None:
                    total = value if positive else -value
                else:
                    total = total + value if positive else total - value
            sums.append(total)
    return sums


def stiffness_kernel(
    state_ref, blocks_ref,
    v_ref, w_ref, f_ref, field_ref, load_ref, edge_ref,
):
    columns, depth = state_ref.shape[1:]
    flags_at, cons_at, moduli_at, sizes_at = 48, 56, 64, 66
    sizes = [state_ref[sizes_at + d] for d in range(3)]
    inverse = [1.0 / size for size in sizes]
    volume = sizes[0] * sizes[1] * sizes[2] * np.float32(0.125)
    bulk, shear = state_ref[moduli_at], state_ref[moduli_at + 1]
    lame = bulk - np.float32(2.0 / 3.0) * shear
    slope = np.float32(3.0 / (CRITICAL_SLOPE * CRITICAL_SLOPE))

    for gauss_index in range(8):
        stress = [state_ref[8 * k + gauss_index] for k in range(6)]
        cons = state_ref[cons_at + gauss_index]
        pressure = (stress[0] + stress[1] + stress[2]) * np.float32(-1.0 / 3.0)
        volumetric = (2.0 * pressure - cons) * np.float32(1.0 / 3.0)
        normal = [slope * (stress[k] + pressure) - volumetric for k in range(3)]
        normal = normal + [(2.0 * slope) * stress[k] for k in range(3, 6)]
        trace = lame * (normal[0] + normal[1] + normal[2])
        twice = 2.0 * shear
        image = [trace + twice * normal[k] for k in range(3)]
        image = image + [shear * normal[k] for k in range(3, 6)]
        denominator = np.float32(HARDENING) * cons * cons
        for k in range(6):
            denominator = denominator + normal[k] * image[k]
        factor = state_ref[flags_at + gauss_index] * volume / denominator
        fields = [[image[VOIGT[i][d]] * inverse[d] for d in range(3)] for i in range(3)]
        for index, value in enumerate(corner_sums(fields, gauss_index)):
            v_ref[gauss_index, index] = value
            w_ref[gauss_index, index] = value * factor
        fields = [[stress[VOIGT[i][d]] * (inverse[d] * volume) for d in range(3)] for i in range(3)]
        for index, value in enumerate(corner_sums(fields, gauss_index)):
            f_ref[index] = value if gauss_index == 0 else f_ref[index] + value

    pair_scale = {}
    for i in range(3):
        for j in range(i, 3):
            scale = volume * inverse[i] * inverse[j]
            pair_scale[i, j] = pair_scale[j, i] = (lame * scale, shear * scale)

    def entry(a, i, b, j):
        terms = [(MOMENTS[a, i, b, j], pair_scale[i, j][0])]
        if i == j:
            for d in range(3):
                weight = MOMENTS[a, d, b, d] + (MOMENTS[a, i, b, i] if d == i else 0.0)
                terms.append((weight, pair_scale[d, d][1]))
        else:
            terms.append((MOMENTS[a, j, b, i], pair_scale[i, j][1]))
        total = combine(terms)
        for gauss_index in range(8):
            term = w_ref[gauss_index, 3 * a + i] * v_ref[gauss_index, 3 * b + j]
            total = -term if total is None else total - term
        return total

    lane = lax.broadcasted_iota(jnp.int32, (columns, depth), 1)
    row = lax.broadcasted_iota(jnp.int32, (columns, depth), 0)
    zero = jnp.zeros((columns, depth), jnp.float32)
    span = depth // PARTS
    live = jnp.where(lax.axis_index("dom") < lax.axis_size("dom") - 1, 1.0, 0.0)

    def along(value):
        return jnp.where(lane == 0, 0.0, pltpu.roll(value, 1, 1))

    def diagonals(p, q, step, other):
        (ax, i), (bx, j) = LINES[p], LINES[q]
        a, b = 4 * ax + 2 * step, 4 * bx + 2 * other
        main = entry(a, i, b, j) + along(entry(a + 1, i, b + 1, j))
        after = along(entry(a, i, b + 1, j))
        if step == other and p == q:
            found = [main * np.float32(0.5), after, zero]
        else:
            found = [main, after, jnp.where(lane == depth - 1, 0.0, entry(a + 1, i, b, j))]
        return [value * live for value in found] if ax or bx else found

    def all_rows(low, high):
        return low + jnp.where(row == 0, 0.0, pltpu.roll(high, 1, 0)), high

    part_of = lane // span

    def regrouped(values):
        moved = [values[0]] + [pltpu.roll(values[q], q * span, 1) for q in range(1, PARTS)]
        parts = []
        for part in range(PARTS):
            merged = moved[-part % PARTS]
            for at in range(1, PARTS):
                merged = jnp.where(part_of == at, moved[(at - part) % PARTS], merged)
            parts.append(pltpu.roll(merged, depth - part * span, 1) if part else merged)
        return parts

    def store(ref, at, kinds):
        for k, pairs in enumerate(kinds):
            firsts = regrouped([zero if pair is None else pair[0] for pair in pairs])
            for part in range(PARTS):
                ref[at + k, part, 0:columns] = firsts[part]
        if all(pair is None or pair[1] is None for pairs in kinds for pair in pairs):
            for k in range(len(kinds)):
                for part in range(PARTS):
                    ref[at + k, part, columns : columns + 1] = zero[0:1]
            return
        lasts = []
        for field in range(PARTS):
            merged = zero
            for k, pairs in enumerate(kinds):
                pair = pairs[field]
                if pair is not None and pair[1] is not None:
                    merged = jnp.where(row == k, pltpu.roll(pair[1], 1 + k, 0), merged)
            lasts.append(merged)
        lasts = regrouped(lasts)
        for k in range(len(kinds)):
            for part in range(PARTS):
                ref[at + k, part, columns : columns + 1] = lasts[part][k : k + 1]

    empty = set()
    for p in range(6):
        for g, slots in enumerate(SLOTS):
            kinds = [[], [], []]
            for following, q in slots:
                if following:
                    values = [(value, None) for value in diagonals(p, q, 0, 1)]
                elif q >= p:
                    low, high = diagonals(p, q, 0, 0), diagonals(p, q, 1, 1)
                    values = [all_rows(low[k], high[k]) for k in range(3)]
                else:
                    values = [None] * 3
                for k in range(3):
                    kinds[k].append(values[k])
            if all(value is None for value in kinds[0]):
                empty.add((p, g))
                continue
            store(field_ref, (p * 3 + g) * 3, kinds)
    loads = []
    for x, d in LINES:
        parts = [f_ref[12 * x + 6 * s + d] + along(f_ref[12 * x + 6 * s + 3 + d]) for s in range(2)]
        loads.append(all_rows(*[part * live for part in parts] if x else parts))
    store(load_ref, 0, [loads[0:4], loads[4:6] + [None, None]])

    place = lax.rem(lax.broadcasted_iota(jnp.int32, (span, depth), 1), span)
    offset = (place - lax.broadcasted_iota(jnp.int32, (span, depth), 0)).astype(jnp.bfloat16)
    is_main, is_after, is_before = offset == 0, offset == 1, offset == -1
    begins = place[0:1] == 0
    ends = place[0:1] == span - 1
    tile_row = lax.broadcasted_iota(jnp.int32, (TILE, depth), 0)
    edge_at = 6 * span
    load_at = edge_at + TILE
    edge_ref[...] = jnp.zeros_like(edge_ref)

    @pl.loop(0, columns + 1, unroll=True)
    def _(y):
        for part in range(PARTS):
            at = y * PARTS + part
            for g in range(len(SLOTS)):
                lanes = slice(g * depth, (g + 1) * depth)
                for p in range(6):
                    rows = slice(p * span, (p + 1) * span)
                    if (p, g) in empty:
                        blocks_ref[at, rows, lanes] = jnp.zeros((span, depth), jnp.bfloat16)
                        continue
                    main, after, before = [
                        field_ref[(p * 3 + g) * 3 + k, part, pl.ds(y, 1), :] for k in range(3)
                    ]
                    main16, after16, before16 = [
                        jnp.broadcast_to(value, (TILE, depth)).astype(jnp.bfloat16)
                        for value in (main, after, before)
                    ]
                    for first in range(0, span, TILE):
                        here = slice(first, first + TILE)
                        blocks_ref[at, p * span + first : p * span + first + TILE, lanes] = jnp.where(
                            is_main[here],
                            main16,
                            jnp.where(
                                is_after[here],
                                after16,
                                jnp.where(is_before[here], before16, jnp.bfloat16(0)),
                            ),
                        )
                    edge_ref[p : p + 1, lanes] = jnp.where(begins, after, 0.0)
                    edge_ref[TILE // 2 + p : TILE // 2 + p + 1, lanes] = jnp.where(ends, before, 0.0)
                if g < 2:
                    value = load_ref[g, part, pl.ds(y, 1), :]
                    leading = value.astype(jnp.bfloat16).astype(jnp.float32)
                    blocks_ref[at, load_at : load_at + TILE, lanes] = jnp.where(
                        tile_row == 0, leading, jnp.where(tile_row == 1, value - leading, 0.0)
                    ).astype(jnp.bfloat16)
                else:
                    blocks_ref[at, load_at : load_at + TILE, lanes] = jnp.zeros((TILE, depth), jnp.bfloat16)
            blocks_ref[at, edge_at:load_at] = edge_ref[...].astype(jnp.bfloat16)


def contract(y, planes, depth, blocks_ref, gather_ref, carry_in, carry_out, total):
    modes = total.shape[1]
    span = depth // PARTS
    own_lanes = lax.broadcasted_iota(jnp.int32, (modes, depth), 1) < 2 * span
    nothing = jnp.zeros((8, modes), jnp.float32)

    def rows(p, first, count):
        ref, at = planes[p // 3]
        start = (p % 3) * depth + first
        return ref[at, start : start + count]

    for border in range(1, PARTS):
        for p in range(6):
            around = rows(p, border * span - TILE, 2 * TILE).astype(jnp.float32)
            at = ((border - 1) * 8 + p) * TILE
            gather_ref[at : at + TILE] = around[TILE // 2 : TILE + TILE // 2]
    for part in range(PARTS):
        before, after = nothing, nothing
        if part > 0:
            before = gather_ref[pl.ds((part - 1) * 8 * TILE + TILE // 2 - 1, 8, TILE)]
        if part < PARTS - 1:
            after = gather_ref[pl.ds(part * 8 * TILE + TILE // 2, 8, TILE)]
        edges = jnp.concatenate([before, after], 0).astype(jnp.bfloat16)
        here = jnp.concatenate([rows(p, part * span, span) for p in range(6)], 0)
        turned = jnp.concatenate([here, edges], 0).T
        at = y * PARTS + part
        product = jnp.dot(
            turned, blocks_ref[at, 0 : 6 * span + TILE], preferred_element_type=jnp.float32
        )
        first = product[:, 0:depth]
        middle = second = product[:, depth : 2 * depth]
        if carry_in is not None:
            first = first + carry_in[part, 0]
            second = second + carry_in[part, 1]
        second = jnp.where(own_lanes, second, 0.0)
        if carry_out is not None:
            carry_out[part, 0] = product[:, 2 * depth :]
            carry_out[part, 1] = pltpu.roll(middle, 2 * span, 1)
        factors = jnp.concatenate([first, second], 1).astype(jnp.bfloat16)
        factors = jnp.concatenate(
            [factors, blocks_ref[at, 6 * span + TILE : 6 * span + 2 * TILE, 0 : 2 * depth]], 0
        )
        total = total + jnp.dot(
            factors[:, 0 : 6 * span], here, preferred_element_type=jnp.float32
        )
    return total


def contraction_kernel(own_ref, front_ref, blocks_ref, sum_ref, carry_ref, gather_ref):
    columns, plane_rows, modes = own_ref.shape
    gather_ref[...] = jnp.zeros_like(gather_ref)
    total = jnp.zeros(sum_ref.shape, jnp.float32)
    for y in range(columns):
        planes = ((own_ref, y), (front_ref, y))
        carried = carry_ref if y else None
        total = contract(
            y, planes, plane_rows // 3, blocks_ref, gather_ref, carried, carry_ref, total
        )
    sum_ref[...] = total


def last_kernel(
    side_ref, corner_ref, blocks_ref, sum_in, carry_in, packed_ref,
    gather_ref, ends_ref,
):
    inside = lax.axis_index("sub") < lax.axis_size("sub") - 1
    ends_ref[0:1] = jnp.where(inside, side_ref[...], jnp.bfloat16(0))
    inside = inside & (lax.axis_index("dom") < lax.axis_size("dom") - 1)
    ends_ref[1:2] = jnp.where(inside, corner_ref[...], jnp.bfloat16(0))
    ignored, plane_rows, modes = side_ref.shape
    columns = blocks_ref.shape[0] // PARTS - 1
    gather_ref[...] = jnp.zeros_like(gather_ref)
    planes = ((ends_ref, 0), (ends_ref, 1))
    total = contract(
        columns, planes, plane_rows // 3, blocks_ref, gather_ref, carry_in, None, sum_in[...]
    )
    upper = total[0:modes]
    tangent = upper + upper.T
    packed_ref[...] = packed(tangent, total[modes : modes + 1] + total[modes + 1 : modes + 2])


def rolled_rows(value, step):
    row = lax.broadcasted_iota(jnp.int32, value.shape, 0)
    result = value
    for j in range(1, value.shape[0]):
        result = jnp.where(row == j, pltpu.roll(value, j * step % value.shape[1], 1), result)
    return result


def packed(tangent, residual):
    modes = tangent.shape[0]
    size = modes // 4
    lane = lax.broadcasted_iota(jnp.int32, (size, modes), 1)
    first, second, third, fourth = [tangent[size * k : size * (k + 1)] for k in range(4)]
    second = jnp.where(lane < size, pltpu.roll(fourth, size, 1), second)
    folded = size // 2
    third = jnp.where(
        lane[:folded] < 2 * size, pltpu.roll(third[folded:], 2 * size, 1), third[:folded]
    )
    count = 2 * modes // size
    spread = rolled_rows(jnp.broadcast_to(residual, (count, modes)), modes - folded)
    middle = jnp.where(lane[:count] < folded, spread, first[folded : folded + count])
    return jnp.concatenate([first[:folded], middle, first[folded + count :], second, third], 0)


def unpack_kernel(mine_ref, other_ref, tangent_ref, residual_ref, packed_ref):
    modes = tangent_ref.shape[0]
    size = modes // 4
    folded = size // 2
    count = 2 * modes // size
    packed_ref[...] = mine_ref[...] + other_ref[...]
    second, third = packed_ref[size : 2 * size], packed_ref[2 * size :]
    upper = jnp.concatenate(
        [
            packed_ref[0 : 2 * size],
            third,
            pltpu.roll(third, 2 * size, 1),
            pltpu.roll(second, modes - size, 1),
        ],
        0,
    )
    lane = lax.broadcasted_iota(jnp.int32, (modes, modes), 1)
    row = lax.broadcasted_iota(jnp.int32, (modes, modes), 0)
    replaced = (row >= folded) & (row < folded + count) & (lane < folded)
    tangent_ref[...] = jnp.where((row // size > lane // size) | replaced, upper.T, upper)
    spread = rolled_rows(packed_ref[folded : folded + count], folded)
    kept = lane[:count] // folded == row[:count]
    residual_ref[...] = jnp.sum(jnp.where(kept, spread, 0.0), axis=0, keepdims=True)


def on_device(
    reduced_basis, gauss_stress, yield_flags, consolidation, elastic_moduli, element_sizes
):
    columns = reduced_basis.shape[1]
    depth, modes = reduced_basis.shape[3], reduced_basis.shape[4]
    plane_rows = 3 * depth
    own = reduced_basis.reshape(columns, plane_rows, modes)
    doms, subs = lax.axis_size("dom"), lax.axis_size("sub")
    front = lax.ppermute(own, "dom", [(s, (s - 1) % doms) for s in range(doms)])
    first = own[0:1]
    corner = lax.ppermute(
        first,
        ("sub", "dom"),
        [
            (s * doms + t, (s - 1) % subs * doms + (t - 1) % doms)
            for s in range(subs)
            for t in range(doms)
        ],
    )
    side = lax.ppermute(first, "sub", [(s, (s - 1) % subs) for s in range(subs)])
    shape = (columns, depth)
    block_rows = 6 * (depth // PARTS) + 2 * TILE
    blocks_shape = ((columns + 1) * PARTS, block_rows, len(SLOTS) * depth)
    fields = [
        value.reshape((-1,) + shape)
        for value in (gauss_stress, yield_flags, consolidation, elastic_moduli, element_sizes)
    ]
    count = sum(value.shape[0] for value in fields)
    state, at = 0.0, 0
    for value in fields:
        end = at + value.shape[0]
        state = state + jnp.pad(value, ((at, count - end), (0, 0), (0, 0))).astype(jnp.float32)
        at = end
    whole = pl.BlockSpec(memory_space=pltpu.VMEM)
    blocks = pl.pallas_call(
        stiffness_kernel,
        out_shape=jax.ShapeDtypeStruct(blocks_shape, jnp.bfloat16),
        in_specs=[whole],
        out_specs=whole,
        scratch_shapes=[
            pltpu.VMEM((8, 24) + shape, jnp.float32),
            pltpu.VMEM((8, 24) + shape, jnp.float32),
            pltpu.VMEM((24,) + shape, jnp.float32),
            pltpu.VMEM((9 * 6, PARTS, 2 * columns, depth), jnp.float32),
            pltpu.VMEM((2, PARTS, 2 * columns, depth), jnp.float32),
            pltpu.VMEM((TILE, len(SLOTS) * depth), jnp.float32),
        ],
        compiler_params=pltpu.CompilerParams(vmem_limit_bytes=24 * 2**20),
        cost_estimate=pl.CostEstimate(flops=20_000_000, bytes_accessed=8_000_000, transcendentals=0),
    )(state)
    packed_rows = modes * 5 // 8
    gather_scratch = pltpu.VMEM(((PARTS - 1) * 8 * TILE + TILE, modes), jnp.float32)
    sum_shape = jax.ShapeDtypeStruct((modes + TILE, modes), jnp.float32)
    carry_shape = jax.ShapeDtypeStruct((PARTS, 2, modes, depth), jnp.float32)
    partial, carry = pl.pallas_call(
        contraction_kernel,
        out_shape=(sum_shape, carry_shape),
        in_specs=[whole] * 3,
        out_specs=(whole, whole),
        scratch_shapes=[gather_scratch],
        compiler_params=pltpu.CompilerParams(vmem_limit_bytes=24 * 2**20),
        cost_estimate=pl.CostEstimate(flops=2_000_000_000, bytes_accessed=8_000_000, transcendentals=0),
    )(own, front, blocks)
    mine = pl.pallas_call(
        last_kernel,
        out_shape=jax.ShapeDtypeStruct((packed_rows, modes), jnp.float32),
        in_specs=[whole] * 5,
        out_specs=whole,
        scratch_shapes=[
            gather_scratch,
            pltpu.VMEM((2, plane_rows, modes), jnp.bfloat16),
        ],
        compiler_params=pltpu.CompilerParams(vmem_limit_bytes=24 * 2**20),
        cost_estimate=pl.CostEstimate(flops=200_000_000, bytes_accessed=1_000_000, transcendentals=0),
    )(side, corner, blocks, partial, carry)

    for axis, first in (("sub", 1), ("dom", 2)):
        for stride, radix in stages(first, lax.axis_size(axis)):
            received = [exchanged(mine, axis, stride * k) for k in ORDERS[axis, radix]]
            mine = sum(received, mine)
    other = exchanged(mine, "dom", 1)
    tangent, residual = pl.pallas_call(
        unpack_kernel,
        out_shape=(
            jax.ShapeDtypeStruct((modes, modes), jnp.float32),
            jax.ShapeDtypeStruct((1, modes), jnp.float32),
        ),
        in_specs=[whole] * 2,
        out_specs=(whole, whole),
        scratch_shapes=[pltpu.VMEM((packed_rows, modes), jnp.float32)],
        compiler_params=pltpu.CompilerParams(vmem_limit_bytes=8 * 2**20),
    )(mine, other)
    return (tangent, residual.reshape(modes))


def exchanged(value, axis, distance):
    return lax.ppermute(value, axis, [(s, s ^ distance) for s in range(lax.axis_size(axis))])


def stages(stride, size):
    first = stride

    found = []
    while stride < size:
        radix = min(4, size // stride)
        found.append((stride, radix))
        stride *= radix
    return found


def solution(mesh):
    return jax.shard_map(
        on_device,
        mesh=mesh,
        in_specs=(
            P("dom", "sub", None, None, None),
            P(None, None, "dom", "sub", None),
            P(None, "dom", "sub", None),
            P(None, "dom", "sub", None),
            P(None, "dom", "sub", None),
            P(None, "dom", "sub", None),
        ),
        out_specs=(P(), P()),
        check_vma=False,
    )
```

```python
import functools

import jax
import jax.numpy as jnp
import numpy as np
from jax import lax
from jax.experimental import pallas as pl
from jax.experimental.pallas import tpu as pltpu
from jax.sharding import PartitionSpec as P

GAUSS_POINT = 0.5773502691896258
CRITICAL_SLOPE = 1.2
HARDENING = 0.5
VOIGT = ((0, 3, 5), (3, 1, 4), (5, 4, 2))
LINES = [(x, d) for x in range(2) for d in range(3)]
SLOTS = [
    [(0, 0), (0, 1), (0, 2), (0, 3)],
    [(0, 4), (0, 5), (1, 4), (1, 5)],
    [(1, 0), (1, 1), (1, 2), (1, 3)],
]
TILE = 16
PARTS = 4
ORDERS = {("sub", 2): (1,), ("sub", 4): (3, 1, 2), ("dom", 2): (1,), ("dom", 4): (2, 3, 1)}


def corner_bits(corner):
    return (corner // 4, corner // 2 % 2, corner % 2)


def derivative_table():
    entries = np.zeros((8, 8, 3))
    for gauss_index in range(8):
        gauss_coords = [GAUSS_POINT * (2 * bit_value - 1) for bit_value in corner_bits(gauss_index)]
        for corner in range(8):
            corner_signs = [2 * bit_value - 1 for bit_value in corner_bits(corner)]
            for axis_index in range(3):
                entry_value = float(corner_signs[axis_index])
                for other_axis in range(3):
                    if other_axis != axis_index:
                        entry_value = (
                            entry_value
                            * (1.0 + corner_signs[other_axis] * gauss_coords[other_axis])
                            / 2.0
                        )
                entries[gauss_index, corner, axis_index] = entry_value
    return entries


TABLE = derivative_table()
MOMENTS = np.einsum("gad,gbe->adbe", TABLE, TABLE)


def combine(terms):
    total = None
    for constant, field in terms:
        if abs(constant) < 1e-14:
            continue
        term = field * np.float32(constant)
        total = term if total is None else total + term
    return total


def corner_sums(fields, gauss_index):
    scaled = {}

    def part(i, d, corner):
        constant = TABLE[gauss_index, corner, d]
        key = (i, d, round(abs(constant), 9))
        if key not in scaled:
            scaled[key] = fields[i][d] * np.float32(abs(constant))
        return scaled[key], constant > 0

    sums = []
    for corner in range(8):
        for i in range(3):
            pieces = sorted((part(i, d, corner) for d in range(3)), key=lambda piece: not piece[1])
            total = None
            for value, positive in pieces:
                if total is None:
                    total = value if positive else -value
                else:
                    total = total + value if positive else total - value
            sums.append(total)
    return sums


def stiffness_kernel(
    state_ref, blocks_ref,
    v_ref, w_ref, f_ref, field_ref, load_ref, edge_ref,
):
    columns, depth = state_ref.shape[1:]
    flags_at, cons_at, moduli_at, sizes_at = 48, 56, 64, 66
    sizes = [state_ref[sizes_at + d] for d in range(3)]
    inverse = [1.0 / size for size in sizes]
    volume = sizes[0] * sizes[1] * sizes[2] * np.float32(0.125)
    bulk, shear = state_ref[moduli_at], state_ref[moduli_at + 1]
    lame = bulk - np.float32(2.0 / 3.0) * shear
    slope = np.float32(3.0 / (CRITICAL_SLOPE * CRITICAL_SLOPE))

    for gauss_index in range(8):
        stress = [state_ref[8 * k + gauss_index] for k in range(6)]
        cons = state_ref[cons_at + gauss_index]
        pressure = (stress[0] + stress[1] + stress[2]) * np.float32(-1.0 / 3.0)
        volumetric = (2.0 * pressure - cons) * np.float32(1.0 / 3.0)
        normal = [slope * (stress[k] + pressure) - volumetric for k in range(3)]
        normal = normal + [(2.0 * slope) * stress[k] for k in range(3, 6)]
        trace = lame * (normal[0] + normal[1] + normal[2])
        twice = 2.0 * shear
        image = [trace + twice * normal[k] for k in range(3)]
        image = image + [shear * normal[k] for k in range(3, 6)]
        denominator = np.float32(HARDENING) * cons * cons
        for k in range(6):
            denominator = denominator + normal[k] * image[k]
        factor = state_ref[flags_at + gauss_index] * volume / denominator
        fields = [[image[VOIGT[i][d]] * inverse[d] for d in range(3)] for i in range(3)]
        for index, value in enumerate(corner_sums(fields, gauss_index)):
            v_ref[gauss_index, index] = value
            w_ref[gauss_index, index] = value * factor
        fields = [[stress[VOIGT[i][d]] * (inverse[d] * volume) for d in range(3)] for i in range(3)]
        for index, value in enumerate(corner_sums(fields, gauss_index)):
            f_ref[index] = value if gauss_index == 0 else f_ref[index] + value

    pair_scale = {}
    for i in range(3):
        for j in range(i, 3):
            scale = volume * inverse[i] * inverse[j]
            pair_scale[i, j] = pair_scale[j, i] = (lame * scale, shear * scale)

    def entry(a, i, b, j):
        terms = [(MOMENTS[a, i, b, j], pair_scale[i, j][0])]
        if i == j:
            for d in range(3):
                weight = MOMENTS[a, d, b, d] + (MOMENTS[a, i, b, i] if d == i else 0.0)
                terms.append((weight, pair_scale[d, d][1]))
        else:
            terms.append((MOMENTS[a, j, b, i], pair_scale[i, j][1]))
        total = combine(terms)
        for gauss_index in range(8):
            term = w_ref[gauss_index, 3 * a + i] * v_ref[gauss_index, 3 * b + j]
            total = -term if total is None else total - term
        return total

    lane = lax.broadcasted_iota(jnp.int32, (columns, depth), 1)
    row = lax.broadcasted_iota(jnp.int32, (columns, depth), 0)
    zero = jnp.zeros((columns, depth), jnp.float32)
    span = depth // PARTS
    live = jnp.where(lax.axis_index("dom") < lax.axis_size("dom") - 1, 1.0, 0.0)

    def along(value):
        return jnp.where(lane == 0, 0.0, pltpu.roll(value, 1, 1))

    def diagonals(p, q, step, other):
        (ax, i), (bx, j) = LINES[p], LINES[q]
        a, b = 4 * ax + 2 * step, 4 * bx + 2 * other
        main = entry(a, i, b, j) + along(entry(a + 1, i, b + 1, j))
        after = along(entry(a, i, b + 1, j))
        if step == other and p == q:
            found = [main * np.float32(0.5), after, zero]
        else:
            found = [main, after, jnp.where(lane == depth - 1, 0.0, entry(a + 1, i, b, j))]
        return [value * live for value in found] if ax or bx else found

    def all_rows(low, high):
        return low + jnp.where(row == 0, 0.0, pltpu.roll(high, 1, 0)), high

    part_of = lane // span

    def regrouped(values):
        moved = [values[0]] + [pltpu.roll(values[q], q * span, 1) for q in range(1, PARTS)]
        parts = []
        for part in range(PARTS):
            merged = moved[-part % PARTS]
            for at in range(1, PARTS):
                merged = jnp.where(part_of == at, moved[(at - part) % PARTS], merged)
            parts.append(pltpu.roll(merged, depth - part * span, 1) if part else merged)
        return parts

    def store(ref, at, kinds):
        for k, pairs in enumerate(kinds):
            firsts = regrouped([zero if pair is None else pair[0] for pair in pairs])
            for part in range(PARTS):
                ref[at + k, part, 0:columns] = firsts[part]
        if all(pair is None or pair[1] is None for pairs in kinds for pair in pairs):
            for k in range(len(kinds)):
                for part in range(PARTS):
                    ref[at + k, part, columns : columns + 1] = zero[0:1]
            return
        lasts = []
        for field in range(PARTS):
            merged = zero
            for k, pairs in enumerate(kinds):
                pair = pairs[field]
                if pair is not None and pair[1] is not None:
                    merged = jnp.where(row == k, pltpu.roll(pair[1], 1 + k, 0), merged)
            lasts.append(merged)
        lasts = regrouped(lasts)
        for k in range(len(kinds)):
            for part in range(PARTS):
                ref[at + k, part, columns : columns + 1] = lasts[part][k : k + 1]

    empty = set()
    for p in range(6):
        for g, slots in enumerate(SLOTS):
            kinds = [[], [], []]
            for following, q in slots:
                if following:
                    values = [(value, None) for value in diagonals(p, q, 0, 1)]
                elif q >= p:
                    low, high = diagonals(p, q, 0, 0), diagonals(p, q, 1, 1)
                    values = [all_rows(low[k], high[k]) for k in range(3)]
                else:
                    values = [None] * 3
                for k in range(3):
                    kinds[k].append(values[k])
            if all(value is None for value in kinds[0]):
                empty.add((p, g))
                continue
            store(field_ref, (p * 3 + g) * 3, kinds)
    loads = []
    for x, d in LINES:
        parts = [f_ref[12 * x + 6 * s + d] + along(f_ref[12 * x + 6 * s + 3 + d]) for s in range(2)]
        loads.append(all_rows(*[part * live for part in parts] if x else parts))
    store(load_ref, 0, [loads[0:4], loads[4:6] + [None, None]])

    place = lax.rem(lax.broadcasted_iota(jnp.int32, (span, depth), 1), span)
    offset = (place - lax.broadcasted_iota(jnp.int32, (span, depth), 0)).astype(jnp.bfloat16)
    is_main, is_after, is_before = offset == 0, offset == 1, offset == -1
    begins = place[0:1] == 0
    ends = place[0:1] == span - 1
    tile_row = lax.broadcasted_iota(jnp.int32, (TILE, depth), 0)
    edge_at = 6 * span
    load_at = edge_at + TILE
    edge_ref[...] = jnp.zeros_like(edge_ref)

    @pl.loop(0, columns + 1, unroll=True)
    def _(y):
        for part in range(PARTS):
            at = y * PARTS + part
            for g in range(len(SLOTS)):
                lanes = slice(g * depth, (g + 1) * depth)
                for p in range(6):
                    rows = slice(p * span, (p + 1) * span)
                    if (p, g) in empty:
                        blocks_ref[at, rows, lanes] = jnp.zeros((span, depth), jnp.bfloat16)
                        continue
                    main, after, before = [
                        field_ref[(p * 3 + g) * 3 + k, part, pl.ds(y, 1), :] for k in range(3)
                    ]
                    main16, after16, before16 = [
                        jnp.broadcast_to(value, (TILE, depth)).astype(jnp.bfloat16)
                        for value in (main, after, before)
                    ]
                    for first in range(0, span, TILE):
                        here = slice(first, first + TILE)
                        blocks_ref[at, p * span + first : p * span + first + TILE, lanes] = jnp.where(
                            is_main[here],
                            main16,
                            jnp.where(
                                is_after[here],
                                after16,
                                jnp.where(is_before[here], before16, jnp.bfloat16(0)),
                            ),
                        )
                    edge_ref[p : p + 1, lanes] = jnp.where(begins, after, 0.0)
                    edge_ref[TILE // 2 + p : TILE // 2 + p + 1, lanes] = jnp.where(ends, before, 0.0)
                if g < 2:
                    value = load_ref[g, part, pl.ds(y, 1), :]
                    leading = value.astype(jnp.bfloat16).astype(jnp.float32)
                    blocks_ref[at, load_at : load_at + TILE, lanes] = jnp.where(
                        tile_row == 0, leading, jnp.where(tile_row == 1, value - leading, 0.0)
                    ).astype(jnp.bfloat16)
                else:
                    blocks_ref[at, load_at : load_at + TILE, lanes] = jnp.zeros((TILE, depth), jnp.bfloat16)
            blocks_ref[at, edge_at:load_at] = edge_ref[...].astype(jnp.bfloat16)


def contract(y, planes, depth, blocks_ref, gather_ref, carry_in, carry_out, total):
    modes = total.shape[1]
    span = depth // PARTS
    own_lanes = lax.broadcasted_iota(jnp.int32, (modes, depth), 1) < 2 * span
    nothing = jnp.zeros((8, modes), jnp.float32)

    def rows(p, first, count):
        ref, at = planes[p // 3]
        start = (p % 3) * depth + first
        return ref[at, start : start + count]

    for border in range(1, PARTS):
        for p in range(6):
            around = rows(p, border * span - TILE, 2 * TILE).astype(jnp.float32)
            at = ((border - 1) * 8 + p) * TILE
            gather_ref[at : at + TILE] = around[TILE // 2 : TILE + TILE // 2]
    for part in range(PARTS):
        before, after = nothing, nothing
        if part > 0:
            before = gather_ref[pl.ds((part - 1) * 8 * TILE + TILE // 2 - 1, 8, TILE)]
        if part < PARTS - 1:
            after = gather_ref[pl.ds(part * 8 * TILE + TILE // 2, 8, TILE)]
        edges = jnp.concatenate([before, after], 0).astype(jnp.bfloat16)
        here = jnp.concatenate([rows(p, part * span, span) for p in range(6)], 0)
        turned = jnp.concatenate([here, edges], 0).T
        at = y * PARTS + part
        product = jnp.dot(
            turned, blocks_ref[at, 0 : 6 * span + TILE], preferred_element_type=jnp.float32
        )
        first = product[:, 0:depth]
        middle = second = product[:, depth : 2 * depth]
        if carry_in is not None:
            first = first + carry_in[part, 0]
            second = second + carry_in[part, 1]
        second = jnp.where(own_lanes, second, 0.0)
        if carry_out is not None:
            carry_out[part, 0] = product[:, 2 * depth :]
            carry_out[part, 1] = pltpu.roll(middle, 2 * span, 1)
        factors = jnp.concatenate([first, second], 1).astype(jnp.bfloat16)
        factors = jnp.concatenate(
            [factors, blocks_ref[at, 6 * span + TILE : 6 * span + 2 * TILE, 0 : 2 * depth]], 0
        )
        total = total + jnp.dot(
            factors[:, 0 : 6 * span], here, preferred_element_type=jnp.float32
        )
    return total


def contract_all(own_ref, front_ref, blocks_ref, sum_ref, carry_ref, gather_ref):
    columns, plane_rows, ignored = own_ref.shape
    gather_ref[...] = jnp.zeros_like(gather_ref)
    total = jnp.zeros(sum_ref.shape, jnp.float32)
    for y in range(columns):
        planes = ((own_ref, y), (front_ref, y))
        carried = carry_ref if y else None
        total = contract(
            y, planes, plane_rows // 3, blocks_ref, gather_ref, carried, carry_ref, total
        )
    sum_ref[...] = total


def on_last_layer():
    return lax.axis_index("dom") == lax.axis_size("dom") - 1


def early_kernel(own_ref, blocks_ref, sum_ref, carry_ref, gather_ref):
    @pl.when(on_last_layer())
    def _():
        contract_all(own_ref, own_ref, blocks_ref, sum_ref, carry_ref, gather_ref)


def contraction_kernel(
    own_ref, front_ref, blocks_ref, sum_early, carry_early, sum_ref, carry_ref, gather_ref
):
    @pl.when(on_last_layer())
    def _():
        sum_ref[...] = sum_early[...]
        carry_ref[...] = carry_early[...]

    @pl.when(jnp.logical_not(on_last_layer()))
    def _():
        contract_all(own_ref, front_ref, blocks_ref, sum_ref, carry_ref, gather_ref)


def last_kernel(
    side_ref, corner_ref, blocks_ref, sum_in, carry_in, packed_ref,
    gather_ref, ends_ref,
):
    inside = lax.axis_index("sub") < lax.axis_size("sub") - 1
    ends_ref[0:1] = jnp.where(inside, side_ref[...], jnp.bfloat16(0))
    inside = inside & (lax.axis_index("dom") < lax.axis_size("dom") - 1)
    ends_ref[1:2] = jnp.where(inside, corner_ref[...], jnp.bfloat16(0))
    ignored, plane_rows, modes = side_ref.shape
    columns = blocks_ref.shape[0] // PARTS - 1
    gather_ref[...] = jnp.zeros_like(gather_ref)
    planes = ((ends_ref, 0), (ends_ref, 1))
    total = contract(
        columns, planes, plane_rows // 3, blocks_ref, gather_ref, carry_in, None, sum_in[...]
    )
    upper = total[0:modes]
    tangent = upper + upper.T
    packed_ref[...] = packed(tangent, total[modes : modes + 1] + total[modes + 1 : modes + 2])


def rolled_rows(value, step):
    row = lax.broadcasted_iota(jnp.int32, value.shape, 0)
    result = value
    for j in range(1, value.shape[0]):
        result = jnp.where(row == j, pltpu.roll(value, j * step % value.shape[1], 1), result)
    return result


def packed(tangent, residual):
    modes = tangent.shape[0]
    size = modes // 4
    lane = lax.broadcasted_iota(jnp.int32, (size, modes), 1)
    first, second, third, fourth = [tangent[size * k : size * (k + 1)] for k in range(4)]
    second = jnp.where(lane < size, pltpu.roll(fourth, size, 1), second)
    folded = size // 2
    third = jnp.where(
        lane[:folded] < 2 * size, pltpu.roll(third[folded:], 2 * size, 1), third[:folded]
    )
    count = 2 * modes // size
    spread = rolled_rows(jnp.broadcast_to(residual, (count, modes)), modes - folded)
    middle = jnp.where(lane[:count] < folded, spread, first[folded : folded + count])
    return jnp.concatenate([first[:folded], middle, first[folded + count :], second, third], 0)


def unpack_kernel(mine_ref, other_ref, tangent_ref, residual_ref, packed_ref):
    modes = tangent_ref.shape[0]
    size = modes // 4
    folded = size // 2
    count = 2 * modes // size
    packed_ref[...] = mine_ref[...] + other_ref[...]
    second, third = packed_ref[size : 2 * size], packed_ref[2 * size :]
    upper = jnp.concatenate(
        [
            packed_ref[0 : 2 * size],
            third,
            pltpu.roll(third, 2 * size, 1),
            pltpu.roll(second, modes - size, 1),
        ],
        0,
    )
    lane = lax.broadcasted_iota(jnp.int32, (modes, modes), 1)
    row = lax.broadcasted_iota(jnp.int32, (modes, modes), 0)
    replaced = (row >= folded) & (row < folded + count) & (lane < folded)
    tangent_ref[...] = jnp.where((row // size > lane // size) | replaced, upper.T, upper)
    spread = rolled_rows(packed_ref[folded : folded + count], folded)
    kept = lane[:count] // folded == row[:count]
    residual_ref[...] = jnp.sum(jnp.where(kept, spread, 0.0), axis=0, keepdims=True)


def on_device(
    reduced_basis, gauss_stress, yield_flags, consolidation, elastic_moduli, element_sizes
):
    columns = reduced_basis.shape[1]
    depth, modes = reduced_basis.shape[3], reduced_basis.shape[4]
    plane_rows = 3 * depth
    own = reduced_basis.reshape(columns, plane_rows, modes)
    doms, subs = lax.axis_size("dom"), lax.axis_size("sub")
    front = lax.ppermute(own, "dom", [(s, (s - 1) % doms) for s in range(doms)])
    first = own[0:1]
    corner = lax.ppermute(
        first,
        ("sub", "dom"),
        [
            (s * doms + t, (s - 1) % subs * doms + (t - 1) % doms)
            for s in range(subs)
            for t in range(doms)
        ],
    )
    side = lax.ppermute(first, "sub", [(s, (s - 1) % subs) for s in range(subs)])
    shape = (columns, depth)
    block_rows = 6 * (depth // PARTS) + 2 * TILE
    blocks_shape = ((columns + 1) * PARTS, block_rows, len(SLOTS) * depth)
    fields = [
        value.reshape((-1,) + shape)
        for value in (gauss_stress, yield_flags, consolidation, elastic_moduli, element_sizes)
    ]
    count = sum(value.shape[0] for value in fields)
    state, at = 0.0, 0
    for value in fields:
        end = at + value.shape[0]
        state = state + jnp.pad(value, ((at, count - end), (0, 0), (0, 0))).astype(jnp.float32)
        at = end
    whole = pl.BlockSpec(memory_space=pltpu.VMEM)
    blocks = pl.pallas_call(
        stiffness_kernel,
        out_shape=jax.ShapeDtypeStruct(blocks_shape, jnp.bfloat16),
        in_specs=[whole],
        out_specs=whole,
        scratch_shapes=[
            pltpu.VMEM((8, 24) + shape, jnp.float32),
            pltpu.VMEM((8, 24) + shape, jnp.float32),
            pltpu.VMEM((24,) + shape, jnp.float32),
            pltpu.VMEM((9 * 6, PARTS, 2 * columns, depth), jnp.float32),
            pltpu.VMEM((2, PARTS, 2 * columns, depth), jnp.float32),
            pltpu.VMEM((TILE, len(SLOTS) * depth), jnp.float32),
        ],
        compiler_params=pltpu.CompilerParams(vmem_limit_bytes=24 * 2**20),
        cost_estimate=pl.CostEstimate(flops=20_000_000, bytes_accessed=8_000_000, transcendentals=0),
    )(state)
    packed_rows = modes * 5 // 8
    gather_scratch = pltpu.VMEM(((PARTS - 1) * 8 * TILE + TILE, modes), jnp.float32)
    sum_shape = jax.ShapeDtypeStruct((modes + TILE, modes), jnp.float32)
    carry_shape = jax.ShapeDtypeStruct((PARTS, 2, modes, depth), jnp.float32)
    settings = {
        "out_shape": (sum_shape, carry_shape),
        "out_specs": (whole, whole),
        "scratch_shapes": [gather_scratch],
        "compiler_params": pltpu.CompilerParams(vmem_limit_bytes=24 * 2**20),
        "cost_estimate": pl.CostEstimate(
            flops=2_000_000_000, bytes_accessed=8_000_000, transcendentals=0
        ),
    }
    early = pl.pallas_call(early_kernel, in_specs=[whole] * 2, **settings)(own, blocks)
    partial, carry = pl.pallas_call(contraction_kernel, in_specs=[whole] * 5, **settings)(
        own, front, blocks, *early
    )
    mine = pl.pallas_call(
        last_kernel,
        out_shape=jax.ShapeDtypeStruct((packed_rows, modes), jnp.float32),
        in_specs=[whole] * 5,
        out_specs=whole,
        scratch_shapes=[
            gather_scratch,
            pltpu.VMEM((2, plane_rows, modes), jnp.bfloat16),
        ],
        compiler_params=pltpu.CompilerParams(vmem_limit_bytes=24 * 2**20),
        cost_estimate=pl.CostEstimate(flops=200_000_000, bytes_accessed=1_000_000, transcendentals=0),
    )(side, corner, blocks, partial, carry)

    for axis, first in (("sub", 1), ("dom", 2)):
        for stride, radix in stages(first, lax.axis_size(axis)):
            received = [exchanged(mine, axis, stride * k) for k in ORDERS[axis, radix]]
            mine = sum(received, mine)
    other = exchanged(mine, "dom", 1)
    tangent, residual = pl.pallas_call(
        unpack_kernel,
        out_shape=(
            jax.ShapeDtypeStruct((modes, modes), jnp.float32),
            jax.ShapeDtypeStruct((1, modes), jnp.float32),
        ),
        in_specs=[whole] * 2,
        out_specs=(whole, whole),
        scratch_shapes=[pltpu.VMEM((packed_rows, modes), jnp.float32)],
        compiler_params=pltpu.CompilerParams(vmem_limit_bytes=8 * 2**20),
    )(mine, other)
    return (tangent, residual.reshape(modes))


def exchanged(value, axis, distance):
    return lax.ppermute(value, axis, [(s, s ^ distance) for s in range(lax.axis_size(axis))])


def stages(stride, size):
    first = stride

    found = []
    while stride < size:
        radix = min(4, size // stride)
        found.append((stride, radix))
        stride *= radix
    return found


def solution(mesh):
    return jax.shard_map(
        on_device,
        mesh=mesh,
        in_specs=(
            P("dom", "sub", None, None, None),
            P(None, None, "dom", "sub", None),
            P(None, "dom", "sub", None),
            P(None, "dom", "sub", None),
            P(None, "dom", "sub", None),
            P(None, "dom", "sub", None),
        ),
        out_specs=(P(), P()),
        check_vma=False,
    )
```
